32 devices in a mesh: row: 8 (over z, x), col: 4 (over y, core).
Axes of the slice: x: 2, y: 2, z: 4, core: 2. Of those that a mesh axis runs over, the one named last changes fastest.
Arguments:
- matrix: bfloat16 [2048, 6144], P('row', 'col'), may hold values from -6 to 6
- pivots: int32 [2, 256], replicated, may hold values from 256 to 2047, as said below
- lower_inverse: bfloat16 [2, 256, 256], replicated, as said below
- upper_inverse: bfloat16 [2, 256, 256], replicated, as said below
Outputs:
- factored: bfloat16 [2048, 6144], P('row', 'col')
The draws below stay inside these ranges and needn't reach their ends.
Inputs may be any that keep to these rules, and one draw needn't show every extreme that they name: Matrix row numbers (not stored rows). Within pivots[s] the entries are distinct and lie in (s + 1) * 256 .. 2047; each step lists (s + 1) * 256 and 2047. Each lower_inverse[s] has ones on the diagonal and zeros above it. Each upper_inverse[s] is zero below the diagonal.
All inputs are finite; a program needn't handle non-finite values.
Results may differ from the reference program's by a relative error of at most 0.0083.
Values may be sent and summed in bfloat16 or wider, within the bound.
No kernel may reach another device: no remote copies, remote signals or barrier semaphores. Data moves between devices by JAX's collectives and lax.ppermute only.
A program may use at most 64 MiB of HBM per device.

```python
import jax
import jax.numpy as jnp
from jax import lax

B = 256
MR = 256
MC = 1536
NR = 2048
NC = 6144
N_ROW = 8
N_COL = 4


def draw_pivots(key, part):
    lists = []
    for step_index in range(2):
        subkey = jax.random.fold_in(key, 11 + step_index)
        lowest = (step_index + 1) * B
        extent = NR - lowest - 2
        ordered = jax.random.permutation(jax.random.fold_in(subkey, 1), extent)[:B - 2] + lowest + 1
        joined = jnp.concatenate([ordered.astype(jnp.int32), jnp.array([lowest, NR - 1], dtype=jnp.int32)])
        shuffled = jax.random.permutation(jax.random.fold_in(subkey, 2), joined)
        lists.append(shuffled.astype(jnp.int32))
    return jnp.stack(lists).astype(jnp.int32)


def draw_lower_inverse(key, part):
    subkey = jax.random.fold_in(key, 21)
    values = jax.random.normal(subkey, (2, B, B), jnp.float32)
    strict = jnp.tril(values, -1) / jnp.sqrt(jnp.float32(B))
    return (strict + jnp.eye(B, dtype=jnp.float32)[None]).astype(jnp.bfloat16)


def draw_upper_inverse(key, part):
    subkey = jax.random.fold_in(key, 31)
    values = jax.random.normal(subkey, (2, B, B), jnp.float32)
    strict = jnp.triu(values, 1) / jnp.sqrt(jnp.float32(B))
    diagonal = jnp.exp(jax.random.uniform(jax.random.fold_in(key, 32), (2, B), jnp.float32, -0.7, 0.7))
    whole = strict + diagonal[:, :, None] * jnp.eye(B, dtype=jnp.float32)[None]
    return (whole / jnp.sqrt(jnp.float32(B))).astype(jnp.bfloat16)


def levels(rng, dims, shards, smallest, high):
    gain = 1.0
    for dim, blocks in shards:
        heights = jax.random.uniform(jax.random.fold_in(jax.random.fold_in(rng, 6), dim), (blocks,), jnp.float32, smallest / len(shards), high / len(shards))
        gain = gain * jnp.repeat(jnp.exp(heights), dims[dim] // blocks).reshape((-1,) + (1,) * (len(dims) - 1 - dim))
    return gain


def gaussian(key, shape, spread, limit, split=(), kind=jnp.bfloat16):
    level = levels(key, shape, split, -0.22, 0.18) if split else 1.0
    values = jax.random.normal(key, shape, jnp.float32) * spread * level
    return jnp.minimum(jnp.maximum(values, -limit), limit).astype(kind)


def setup_inputs(seed: int = 0) -> dict:
    seeds = jax.random.split(jax.random.key(seed), 5)
    return {
        "matrix": gaussian(seeds[0], (NR, NC), 1.0, 6.0, ((0, 8), (1, 4))),
        "pivots": draw_pivots(jax.random.fold_in(seeds[4], 71), 0),
        "lower_inverse": draw_lower_inverse(jax.random.fold_in(seeds[4], 71), 0),
        "upper_inverse": draw_upper_inverse(jax.random.fold_in(seeds[4], 71), 0),
    }


def stored_rows(index):
    blocks = index // B
    return ((blocks % N_ROW) * MR + (blocks // N_ROW) * B + index % B).astype(jnp.int32)


def stored_cols(index):
    blocks = index // B
    return ((blocks % N_COL) * MC + (blocks // N_COL) * B + index % B).astype(jnp.int32)


def reference(matrix, pivots, lower_inverse, upper_inverse):
    row_ids = jnp.arange(NR, dtype=jnp.int32)
    col_ids = jnp.arange(NC, dtype=jnp.int32)
    row_block = ((row_ids % MR) // B) * N_ROW + row_ids // MR
    col_block = ((col_ids % MC) // B) * N_COL + col_ids // MC
    within = jnp.arange(B, dtype=jnp.int32)
    current = matrix
    for step_index in range(2):
        top_rows = stored_rows(step_index * B + within)
        pivot_rows = stored_rows(pivots[step_index].astype(jnp.int32))
        upper_block = current[top_rows]
        picked = current[pivot_rows]
        current = current.at[top_rows].set(picked).at[pivot_rows].set(upper_block)
        row_live = row_block > step_index
        col_live = col_block > step_index
        panel_cols = stored_cols(step_index * B + within)
        panel = jnp.take(current, panel_cols, axis=1).astype(jnp.float32)
        upper_inv = upper_inverse[step_index].astype(jnp.float32)
        lower_all = jnp.dot(panel, upper_inv, precision=lax.Precision.HIGHEST).astype(matrix.dtype)
        lower_all = jnp.where(row_live[:, None], lower_all, jnp.zeros_like(lower_all))
        new_top = current[top_rows].astype(jnp.float32)
        lower_inv = lower_inverse[step_index].astype(jnp.float32)
        upper = jnp.dot(lower_inv, new_top, precision=lax.Precision.HIGHEST).astype(matrix.dtype)
        upper = jnp.where(col_live[None, :], upper, jnp.zeros_like(upper))
        upper_wide = upper.astype(jnp.float32)

        def update(pair):
            rows_here, lower_here = pair
            product = jnp.dot(lower_here.astype(jnp.float32), upper_wide, precision=lax.Precision.HIGHEST)
            return (rows_here.astype(jnp.float32) - product).astype(matrix.dtype)

        stacked = lax.map(update, (current.reshape(N_ROW, MR, NC), lower_all.reshape(N_ROW, MR, B)))
        current = stacked.reshape(NR, NC)
        old_panel = jnp.take(current, panel_cols, axis=1)
        current = current.at[:, panel_cols].set(jnp.where(row_live[:, None], lower_all, old_panel))
        old_top = current[top_rows]
        current = current.at[top_rows].set(jnp.where(col_live[None, :], upper, old_top))
    return current
```

```python
import functools

import jax
import jax.numpy as jnp
from jax import lax
from jax.experimental import pallas as pl
from jax.experimental.pallas import tpu as pltpu
from jax.sharding import PartitionSpec as P

BF = jnp.bfloat16
F32 = jnp.float32
I32 = jnp.int32
VMEM_LIMIT = 32 * 1024 * 1024
WHOLE = pl.BlockSpec(memory_space=pltpu.VMEM)
SCALARS = pl.BlockSpec(memory_space=pltpu.SMEM)
PARAMS = pltpu.CompilerParams(vmem_limit_bytes=VMEM_LIMIT)


def matmul(a, b):
    return jnp.dot(a, b, preferred_element_type=F32)


def rounded(a, b):
    return matmul(a, b).astype(BF)


def call(kernel, out_shape, in_specs, out_specs, *args, aliases=None, scratch=(), flops=1 << 27):
    moved = sum(a.size * a.dtype.itemsize for a in args)
    return pl.pallas_call(
        kernel,
        grid=(1,),
        out_shape=out_shape,
        in_specs=in_specs,
        out_specs=out_specs,
        scratch_shapes=list(scratch),
        input_output_aliases=aliases or {},
        compiler_params=PARAMS,
        cost_estimate=pl.CostEstimate(flops=flops, bytes_accessed=moved, transcendentals=0),
    )(*args)


def pack_kernel(width, chunks, info, source, *outs):
    place = lax.rem(info[0], 4)
    for d in range(4):
        quarter = lax.bitwise_xor(place, d)
        for k in range(chunks):
            start = pl.multiple_of((k * 4 + quarter) * width, 128)
            outs[d][:, k * width : (k + 1) * width] = source[:, pl.ds(start, width)]


def pick(flags, values, axis):
    return jnp.sum(jnp.where(flags, values, 0.0), axis=axis, keepdims=True)


def found(flags, axis):
    return jnp.max(jnp.where(flags, 1.0, 0.0), axis=axis, keepdims=True) > 0.0


def plan_kernel(block, info, flat, tall, src_out, gather_out, displaced_out, mine_out, put_out):
    me = info[0]
    first_row = flat[0:1, :].astype(F32)
    second_row = flat[1:2, :].astype(F32)
    first_col = tall[:, 0:1].astype(F32)
    second_col = tall[:, 1:2].astype(F32)
    shape = (block, block)
    down = lax.broadcasted_iota(I32, shape, 0).astype(F32)
    along = lax.broadcasted_iota(I32, shape, 1).astype(F32)
    size = float(block)
    both = first_col == second_row
    both_turned = second_col == first_row
    inside = first_col == along + size
    inside_turned = first_row == down + size
    moved_row = jnp.where(found(inside, 0), pick(inside, down, 0), along[0:1] + size)
    moved_col = jnp.where(found(inside_turned, 1), pick(inside_turned, along, 1), down[:, 0:1] + size)
    source_row = jnp.where(found(both, 0), pick(both, down, 0), second_row)
    source_col = jnp.where(found(both_turned, 1), pick(both_turned, along, 1), second_col)
    shifted_col = jnp.where(found(both, 1), pick(both, moved_row, 1), down[:, 0:1])
    sources = jnp.concatenate([first_col, source_col], axis=0).astype(I32)
    displaced = jnp.concatenate([shifted_col, moved_col], axis=0).astype(I32)
    source_flat = jnp.concatenate([first_row, source_row], axis=1).astype(I32)
    src_out[...] = sources
    group = me // 4
    owner = sources // block
    here = (owner // 4) == group
    leaves = sources >= 2 * block
    at_home = group == 0
    taken = jnp.where(here, sources, jnp.where(at_home, displaced, -1))
    gone = jnp.where(jnp.logical_and(leaves, at_home), displaced, -1)
    lanes = lax.broadcasted_iota(I32, (2 * block, block), 1)
    for d in range(4):
        base = lax.bitwise_xor(me, d) * block
        cols = slice(d * block, (d + 1) * block)
        gather_out[:, cols] = jnp.where(taken - base == lanes, 1.0, 0.0).astype(BF)
        displaced_out[:, cols] = jnp.where(gone - base == lanes, 1.0, 0.0).astype(BF)
    mine_out[...] = jnp.where(sources - me * block == lanes, 1.0, 0.0).astype(BF)
    rows = lax.broadcasted_iota(I32, (block, 2 * block), 0) + me * block
    slots = lax.broadcasted_iota(I32, (block, 2 * block), 1)
    wanted = jnp.where(me < 2, slots, source_flat)
    put_out[...] = jnp.where(wanted == rows, 1.0, 0.0).astype(BF)


def select_kernel(width, a, b, c, d, gather, displaced, *outs):
    parts = (a, b, c, d)
    block = a.shape[0]
    count = len(outs) // 2
    kept = sum(matmul(gather[:, i * block : (i + 1) * block], parts[i][...]) for i in range(4)).astype(BF)
    gone = sum(matmul(displaced[:, i * block : (i + 1) * block], parts[i][...]) for i in range(4)).astype(BF)
    for k in range(count):
        outs[2 * k][...] = kept[:, k * width : (k + 1) * width]
        outs[2 * k + 1][...] = gone[:, k * width : (k + 1) * width]


def merge_kernel(block, info, src, kept, received, gone, *outs):
    me = info[0]
    side = info[2]
    sources = src[...]
    owner = sources // block
    from_here = (owner // 4) // side == (me // 4) // side
    top = jnp.where(from_here, kept[...], received[...])
    moved = jnp.where((me // 4) // side == 0, gone[...], received[...])
    leaves = sources >= 2 * block
    for d in range(4):
        theirs = jnp.logical_and(owner == lax.bitwise_xor(me, d), leaves)
        outs[d][...] = jnp.where(theirs, moved, top)


def assemble(block, width, me, src, mine, put, messages, raw, top, own):
    place = lax.rem(me, 4)
    owned = (src[...] // block) == me
    vacated = jnp.sum(put[...].astype(F32), axis=1, keepdims=True) > 0.0
    kept = jnp.logical_not(jnp.logical_or(vacated, me < 2))
    for d in range(4):
        start = pl.multiple_of(lax.bitwise_xor(place, d) * width, 128)
        here = raw[:, pl.ds(start, width)]
        message = messages[d][...]
        complete = jnp.where(owned, rounded(mine[...], here), message)
        top[:, pl.ds(start, width)] = complete
        incoming = jnp.where(me < 2, complete, message)
        own[:, pl.ds(start, width)] = jnp.where(kept, here, rounded(put[...], incoming))


def panel_kernel(block, width, info, src, mine, put, m0, m1, m2, m3, raw, low, high, top, own, sent):
    assemble(block, width, info[0], src, mine, put, (m0, m1, m2, m3), raw, top, own)
    high_inverse = high[0]
    head = top[:block, :block]
    below = top[block:, :block]
    here = own[:, :block]

    @pl.when(info[1] == 0)
    def _():
        sent[:block] = rounded(here, high_inverse)
        sent[block:] = rounded(below, high_inverse)

    @pl.when(info[1] != 0)
    def _():
        sent[:block] = here
        sent[block:] = rounded(low[0], head)


def finish(block, info, left, right, low, high, top, own, out, special):
    me = info[0]
    lower_own = left[:block]
    lower_next = left[block:]
    panel = (right[:block].astype(F32) - matmul(lower_own, right[block:])).astype(BF)
    lower_second = rounded(panel, high[1])
    upper = rounded(low[0], top[:block])
    following = (top[block:].astype(F32) - matmul(lower_next, upper)).astype(BF)
    upper_second = rounded(low[1], following)
    once = (own[...].astype(F32) - matmul(lower_own, upper)).astype(BF)
    twice = (once.astype(F32) - matmul(lower_second, upper_second)).astype(BF)
    out[...] = jnp.where(me == 0, upper, jnp.where(me == 1, upper_second, twice))
    if special:
        my_col = info[1]

        @pl.when(my_col == 0)
        def _():
            out[:, :block] = jnp.where(me == 0, top[:block, :block], lower_own)

        @pl.when(my_col == 1)
        def _():
            rest = jnp.where(me == 1, following[:, :block], lower_second)
            out[:, :block] = jnp.where(me == 0, upper[:, :block], rest)


def first_kernel(block, info, left, right, low, high, top, own, out):
    finish(block, info, left[...], right[...], low, high, top[...], own[...], out, True)


def later_kernel(block, width, info, src, mine, put, m0, m1, m2, m3, raw, left, right, low, high, done, out, top, own):
    assemble(block, width, info[0], src, mine, put, (m0, m1, m2, m3), raw, top, own)
    finish(block, info, left[...], right[...], low, high, top[...], own[...], out, False)


def exchange(value, bit):
    size = lax.axis_size("row")
    return lax.ppermute(value, "row", [(i, i ^ bit) for i in range(size)])


def body(matrix, pivots, lower_inverse, upper_inverse):
    rows, cols = matrix.shape
    block = lower_inverse.shape[1]
    grid_rows = lax.axis_size("row")
    grid_cols = lax.axis_size("col")
    my_row = lax.axis_index("row")
    my_col = lax.axis_index("col")
    width = 128
    chunks = cols // (4 * width)
    span = 4 * width
    groups = grid_rows // 4
    last_side = max(groups // 2, 1)
    info = jnp.stack([my_row, my_col, jnp.int32(last_side)]).astype(I32)
    shape = jax.ShapeDtypeStruct

    def block_spec(index):
        return pl.BlockSpec((rows, span), lambda step: (0, index))

    packed = [
        call(
            functools.partial(pack_kernel, width, 1),
            [shape((rows, width), BF)] * 4,
            [SCALARS, WHOLE],
            [WHOLE] * 4,
            info,
            matrix[:, :span],
        ),
        call(
            functools.partial(pack_kernel, width, chunks - 1),
            [shape((rows, (chunks - 1) * width), BF)] * 4,
            [SCALARS, WHOLE],
            [WHOLE] * 4,
            info,
            matrix[:, span:],
        ),
    ]
    gathered = [[p[0]] + [exchange(p[d], d) for d in (1, 2, 3)] for p in packed]

    src, gather, displaced, mine, put = call(
        functools.partial(plan_kernel, block),
        [
            shape((2 * block, 1), I32),
            shape((2 * block, 4 * block), BF),
            shape((2 * block, 4 * block), BF),
            shape((2 * block, block), BF),
            shape((block, 2 * block), BF),
        ],
        [SCALARS, WHOLE, WHOLE],
        [WHOLE] * 5,
        info,
        pivots,
        pivots.T,
    )

    slots = shape((2 * block, width), BF)
    chosen = []
    for part, count in zip(gathered, (1, chunks - 1)):
        outs = call(
            functools.partial(select_kernel, width),
            [slots] * (2 * count),
            [WHOLE] * 6,
            [WHOLE] * (2 * count),
            *part,
            gather,
            displaced,
        )
        chosen += [(outs[2 * k], outs[2 * k + 1]) for k in range(count)]

    owner_group = src // block // 4
    my_group = my_row // 4

    def complete(kept, gone):
        side = 1
        while side < last_side:
            received = exchange(kept, 4 * side)
            here = my_group // side
            owners = owner_group // side
            keep = jnp.logical_or(owners == here, jnp.logical_and(here == 0, owners != 1))
            kept, gone = (
                jnp.where(keep, kept, received),
                jnp.where(here == 1, received, gone),
            )
            side *= 2
        received = exchange(kept, 4 * side)
        messages = call(
            functools.partial(merge_kernel, block),
            [slots] * 4,
            [SCALARS] + [WHOLE] * 4,
            [WHOLE] * 4,
            info,
            src,
            kept,
            received,
            gone,
        )
        return [messages[0]] + [exchange(messages[d], d) for d in (1, 2, 3)]

    messages = [complete(kept, gone) for kept, gone in chosen]

    top, own, sent = call(
        functools.partial(panel_kernel, block, width),
        [shape((2 * block, span), BF), shape((block, span), BF), shape((2 * block, block), BF)],
        [SCALARS] + [WHOLE] * 10,
        [WHOLE] * 3,
        info,
        src,
        mine,
        put,
        *messages[0],
        matrix[:, :span],
        lower_inverse,
        upper_inverse,
    )
    reach = 2
    while reach < grid_cols:
        arrived = lax.ppermute(sent, "col", [(i, i + reach) for i in range(min(reach, grid_cols - reach))])
        sent = jnp.where(jnp.logical_and(my_col >= reach, my_col < 2 * reach), arrived, sent)
        reach *= 2
    other = lax.ppermute(sent, "col", [(i, i ^ 1) for i in range(grid_cols)])
    even = my_col % 2 == 0
    left = jnp.where(even, sent, other)
    right = jnp.where(even, other, sent)

    out = call(
        functools.partial(first_kernel, block),
        shape((rows, cols), BF),
        [SCALARS] + [WHOLE] * 6,
        block_spec(0),
        info,
        left,
        right,
        lower_inverse,
        upper_inverse,
        top,
        own,
    )
    for k in range(1, chunks):
        out = call(
            functools.partial(later_kernel, block, width),
            shape((rows, cols), BF),
            [SCALARS] + [WHOLE] * 7 + [block_spec(k)] + [WHOLE] * 4 + [pl.BlockSpec(memory_space=pl.ANY)],
            block_spec(k),
            info,
            src,
            mine,
            put,
            *messages[k],
            matrix,
            left,
            right,
            lower_inverse,
            upper_inverse,
            out,
            aliases={13: 0},
            scratch=[pltpu.VMEM((2 * block, span), BF), pltpu.VMEM((block, span), BF)],
        )
    return out


def solution(mesh):
    placed = (P("row", "col"), P(), P(), P())
    return jax.shard_map(
        body, mesh=mesh, in_specs=placed, out_specs=P("row", "col"), check_vma=False
    )
```

```python
import functools

import jax
import jax.numpy as jnp
from jax import lax
from jax.experimental import pallas as pl
from jax.experimental.pallas import tpu as pltpu
from jax.sharding import PartitionSpec as P

BF = jnp.bfloat16
F32 = jnp.float32
I32 = jnp.int32
VMEM_LIMIT = 12 * 1024 * 1024
LANES = 128
ANYWHERE = pl.BlockSpec(memory_space=pl.ANY)
WHOLE = pl.BlockSpec(memory_space=pltpu.VMEM)
SCALARS = pl.BlockSpec(memory_space=pltpu.SMEM)
PARAMS = pltpu.CompilerParams(vmem_limit_bytes=VMEM_LIMIT)


def matmul(a, b):
    return jnp.dot(a, b, preferred_element_type=F32)


def rounded(a, b):
    return matmul(a, b).astype(BF)


def call(kernel, out_shape, in_specs, out_specs, *args, after=(), aliases=None, scratch=(), flops=1 << 27):
    moved = sum(a.size * a.dtype.itemsize for a in args)
    used = len(args)

    def ordered(*refs):
        kernel(*refs[:used], *refs[used + len(after) :])

    in_specs = list(in_specs) + [ANYWHERE] * len(after)
    args = args + tuple(after)
    return pl.pallas_call(
        ordered,
        grid=(1,),
        out_shape=out_shape,
        in_specs=in_specs,
        out_specs=out_specs,
        scratch_shapes=list(scratch),
        input_output_aliases=aliases or {},
        compiler_params=PARAMS,
        cost_estimate=pl.CostEstimate(flops=flops, bytes_accessed=moved, transcendentals=0),
    )(*args)


def pack_kernel(chunks, info, source, *outs):
    place = lax.rem(info[0], 4)
    for k, (base, width) in enumerate(chunks):
        for d in range(4):
            start = pl.multiple_of(base + lax.bitwise_xor(place, d) * width, LANES)
            outs[4 * k + d][...] = source[:, pl.ds(start, width)]


def pick(flags, values, axis):
    return jnp.sum(jnp.where(flags, values, 0.0), axis=axis, keepdims=True)


def found(flags, axis):
    return jnp.max(jnp.where(flags, 1.0, 0.0), axis=axis, keepdims=True) > 0.0


def plan_kernel(block, info, flat, tall, src_out, kept_out, gather_out, displaced_out, mine_out, put_out):
    me = info[0]
    first_row = flat[0:1, :].astype(F32)
    second_row = flat[1:2, :].astype(F32)
    first_col = tall[:, 0:1].astype(F32)
    second_col = tall[:, 1:2].astype(F32)
    shape = (block, block)
    down = lax.broadcasted_iota(I32, shape, 0).astype(F32)
    along = lax.broadcasted_iota(I32, shape, 1).astype(F32)
    size = float(block)
    both = first_col == second_row
    both_turned = second_col == first_row
    inside = first_col == along + size
    inside_turned = first_row == down + size
    moved_row = jnp.where(found(inside, 0), pick(inside, down, 0), along[0:1] + size)
    moved_col = jnp.where(found(inside_turned, 1), pick(inside_turned, along, 1), down[:, 0:1] + size)
    source_row = jnp.where(found(both, 0), pick(both, down, 0), second_row)
    source_col = jnp.where(found(both_turned, 1), pick(both_turned, along, 1), second_col)
    shifted_col = jnp.where(found(both, 1), pick(both, moved_row, 1), down[:, 0:1])
    sources = jnp.concatenate([first_col, source_col], axis=0).astype(I32)
    displaced = jnp.concatenate([shifted_col, moved_col], axis=0).astype(I32)
    source_flat = jnp.concatenate([first_row, source_row], axis=1).astype(I32)
    src_out[...] = jnp.broadcast_to(sources, src_out.shape)
    square = me - lax.rem(me, 4)
    here = jnp.logical_and(sources >= square * block, sources < (square + 4) * block)
    leaves = sources >= 2 * block
    at_home = square == 0
    taken = jnp.where(here, sources, jnp.where(at_home, displaced, -1))
    gone = jnp.where(jnp.logical_and(leaves, at_home), displaced, -1)
    lanes = lax.broadcasted_iota(I32, (2 * block, block), 1)
    for d in range(4):
        cols = slice(d * block, (d + 1) * block)
        gather_out[:, cols] = jnp.where(taken - lax.bitwise_xor(me, d) * block == lanes, 1.0, 0.0).astype(BF)
    near = jnp.where(lax.rem(me, 4) < 2, 0, 2)
    for d in range(2):
        cols = slice(d * block, (d + 1) * block)
        base = lax.bitwise_xor(me, near + d) * block
        displaced_out[:, cols] = jnp.where(gone - base == lanes, 1.0, 0.0).astype(BF)
    mine_out[...] = jnp.where(sources - me * block == lanes, 1.0, 0.0).astype(BF)
    rows = lax.broadcasted_iota(I32, (block, 2 * block), 0) + me * block
    put = source_flat == rows
    put_out[...] = jnp.where(put, 1.0, 0.0).astype(BF)
    kept_out[...] = jnp.broadcast_to(jnp.where(found(put, 1), 0, 1), kept_out.shape)


def select_kernel(info, a, b, c, d, gather, displaced, kept, gone, rows):
    block = a.shape[0]
    for i, part in enumerate((a, b, c, d)):
        rows[i * block : (i + 1) * block] = part[...]
    kept[...] = rounded(gather[...], rows[...])
    start = pl.multiple_of(jnp.where(lax.rem(info[0], 4) < 2, 0, 2 * block), 2 * block)
    gone[...] = rounded(displaced[...], rows[pl.ds(start, 2 * block)])


def tiles(width):
    return [slice(i, i + LANES) for i in range(0, width, LANES)]


def merge_kernel(block, info, src, kept, received, gone, *outs):
    me = info[0]
    side = 4 * info[2]
    sources = src[...]
    mine = lax.div(me, side) * side * block
    from_here = jnp.logical_and(sources >= mine, sources < mine + side * block)
    leaves = sources >= 2 * block
    for cols in tiles(kept.shape[1]):
        arrived = received[:, cols].astype(F32)
        top = jnp.where(from_here, kept[:, cols].astype(F32), arrived)
        moved = jnp.where(me < side, gone[:, cols].astype(F32), arrived)
        for d in range(4):
            base = lax.bitwise_xor(me, d) * block
            theirs = jnp.logical_and(jnp.logical_and(sources >= base, sources < base + block), leaves)
            outs[d][:, cols] = jnp.where(theirs, moved, top).astype(BF)


def assemble(block, base, width, me, src, kept, mine, put, messages, raw, slots, top, own):
    place = lax.rem(me, 4)
    span = 4 * width
    for d in range(4):
        start = pl.multiple_of(lax.bitwise_xor(place, d) * width, LANES)
        slots[:, pl.ds(start, width)] = messages[d][...]
    here = raw[:, base : base + span]
    sources = src[...]
    owned = jnp.logical_and(sources >= me * block, sources < (me + 1) * block)
    unmoved = kept[...] > 0
    candidates = matmul(mine[...], here)
    placed = matmul(put[...], slots[...])
    for cols in tiles(span):
        top[:, cols] = jnp.where(owned, candidates[:, cols], slots[:, cols].astype(F32)).astype(BF)
        own[:, cols] = jnp.where(unmoved, here[:, cols].astype(F32), placed[:, cols]).astype(BF)

    @pl.when(me < 2)
    def _():
        own[...] = top[pl.ds(pl.multiple_of(me * block, block), block)]


def panel_kernel(block, base, width, info, src, kept, mine, put, m0, m1, m2, m3, raw, low, high, top, own, sent, more, slots):
    assemble(block, base, width, info[0], src, kept, mine, put, (m0, m1, m2, m3), raw, slots, top, own)

    @pl.when(info[1] == 0)
    def _():
        sent[...] = rounded(own[:, :block], high[0])
        more[...] = rounded(top[block:, :block], high[0])

    @pl.when(info[1] != 0)
    def _():
        sent[...] = own[:, :block]
        more[...] = rounded(low[0], top[:block, :block])


def finish(block, info, lower_own, lower_next, second, head, low, high, top, own, out):
    me = info[0]
    panel = (second[...].astype(F32) - matmul(lower_own[...], head[...])).astype(BF)
    lower_second = rounded(panel, high[1])
    upper = rounded(low[0], top[:block])
    following = (top[block:].astype(F32) - matmul(lower_next[...], upper)).astype(BF)
    upper_second = rounded(low[1], following)
    once = (own[...].astype(F32) - matmul(lower_own[...], upper)).astype(BF)
    out[...] = (once.astype(F32) - matmul(lower_second, upper_second)).astype(BF)

    @pl.when(me == 0)
    def _():
        out[...] = upper

    @pl.when(me == 1)
    def _():
        out[...] = upper_second

    return upper, following, lower_second


def write(result, out, base, done):
    copy = pltpu.make_async_copy(result, out.at[:, pl.ds(base, result.shape[1])], done)
    copy.start()
    copy.wait()


def first_kernel(block, base, info, a, b, c, d, low, high, top, own, out, result, done):
    upper, following, lower_second = finish(block, info, a, b, c, d, low, high, top, own, result)
    me = info[0]

    @pl.when(info[1] == 0)
    def _():
        result[:, :block] = jnp.where(me == 0, top[:block, :block], a[...])

    @pl.when(info[1] == 1)
    def _():
        rest = jnp.where(me == 1, following[:, :block], lower_second)
        result[:, :block] = jnp.where(me == 0, upper[:, :block], rest)

    write(result, out, base, done)


def later_kernel(
    block, base, width, info, src, kept, mine, put, m0, m1, m2, m3, raw, a, b, c, d, low, high, before, out,
    slots, top, own, result, done,
):
    assemble(block, base, width, info[0], src, kept, mine, put, (m0, m1, m2, m3), raw, slots, top, own)
    finish(block, info, a, b, c, d, low, high, top, own, result)
    write(result, out, base, done)


def exchange(value, bit, axis="row"):
    return lax.ppermute(value, axis, [(i, i ^ bit) for i in range(lax.axis_size(axis))])


def body(matrix, pivots, lower_inverse, upper_inverse):
    rows, cols = matrix.shape
    block = lower_inverse.shape[1]
    grid_rows = lax.axis_size("row")
    grid_cols = lax.axis_size("col")
    my_row = lax.axis_index("row")
    my_col = lax.axis_index("col")
    units = cols // (4 * LANES)
    widths = [1, units - 1]
    chunks = []
    base = 0
    for count in widths:
        chunks.append((base, count * LANES))
        base += 4 * count * LANES
    groups = grid_rows // 4
    last_side = max(groups // 2, 1)
    info = jnp.stack([my_row, my_col, jnp.int32(last_side)]).astype(I32)
    shape = jax.ShapeDtypeStruct

    packed = call(
        functools.partial(pack_kernel, chunks),
        [shape((rows, width), BF) for _, width in chunks for _ in range(4)],
        [SCALARS, WHOLE],
        [WHOLE] * (4 * len(chunks)),
        info,
        matrix,
    )
    gathered = [
        [packed[4 * k]] + [exchange(packed[4 * k + d], d) for d in (1, 2, 3)] for k in range(len(chunks))
    ]

    src, kept, gather, displaced, mine, put = call(
        functools.partial(plan_kernel, block),
        [
            shape((2 * block, LANES), I32),
            shape((block, LANES), I32),
            shape((2 * block, 4 * block), BF),
            shape((2 * block, 2 * block), BF),
            shape((2 * block, block), BF),
            shape((block, 2 * block), BF),
        ],
        [SCALARS, WHOLE, WHOLE],
        [WHOLE] * 6,
        info,
        pivots,
        pivots.T,
    )

    owner_group = src[:, :1] // block // 4
    my_group = my_row // 4

    def collect(part, width, after=()):
        slots = shape((2 * block, width), BF)
        return call(
            select_kernel,
            [slots] * 2,
            [SCALARS] + [WHOLE] * 6,
            [WHOLE] * 2,
            info,
            *part,
            gather,
            displaced,
            after=after,
            scratch=[pltpu.VMEM((4 * block, width), BF)],
        )

    def deliver(held, gone, width, after=()):
        side = 1
        while side < last_side:
            received = exchange(held, 4 * side)
            here = my_group // side
            owners = owner_group // side
            keep = jnp.logical_or(owners == here, jnp.logical_and(here == 0, owners != 1))
            held, gone = jnp.where(keep, held, received), jnp.where(here == 1, received, gone)
            side *= 2
        received = exchange(held, 4 * side)
        messages = call(
            functools.partial(merge_kernel, block),
            [shape((2 * block, width), BF)] * 4,
            [SCALARS] + [WHOLE] * 4,
            [WHOLE] * 4,
            info,
            src,
            held,
            received,
            gone,
            after=after,
        )
        return [messages[0]] + [exchange(messages[d], d) for d in (1, 2, 3)]

    collected = []
    for part, (_, width) in zip(gathered, chunks):
        collected.append(collect(part, width))
    first = deliver(*collected[0], chunks[0][1], after=[c[0] for c in collected[1:]])

    base, width = chunks[0]
    span = 4 * width
    top, own, *sent = call(
        functools.partial(panel_kernel, block, base, width),
        [shape((2 * block, span), BF), shape((block, span), BF)] + [shape((block, block), BF)] * 2,
        [SCALARS] + [WHOLE] * 11,
        [WHOLE] * 4,
        info,
        src,
        kept,
        mine,
        put,
        *first,
        matrix,
        lower_inverse,
        upper_inverse,
        scratch=[pltpu.VMEM((2 * block, span), BF)],
    )
    messages = [deliver(*c, width, after=sent[:1]) for c, (_, width) in zip(collected[1:], chunks[1:])]
    reach = 2
    while reach < grid_cols:
        arrived = [exchange(part, reach, "col") for part in sent]
        fresh = jnp.logical_and(my_col >= reach, my_col < 2 * reach)
        sent = [jnp.where(fresh, new, old) for new, old in zip(arrived, sent)]
        reach *= 2
    half = block // 2
    other = [
        jnp.concatenate([exchange(part[:half], 1, "col"), exchange(part[half:], 1, "col")]) for part in sent
    ]
    even = my_col % 2 == 0
    panels = [jnp.where(even, x, y) for x, y in zip(sent, other)] + [jnp.where(even, y, x) for x, y in zip(sent, other)]

    out = call(
        functools.partial(first_kernel, block, base),
        shape((rows, cols), BF),
        [SCALARS] + [WHOLE] * 8,
        ANYWHERE,
        info,
        *panels,
        lower_inverse,
        upper_inverse,
        top,
        own,
        scratch=[pltpu.VMEM((block, span), BF), pltpu.SemaphoreType.DMA],
    )
    for k in range(1, len(chunks)):
        base, width = chunks[k]
        span = 4 * width
        out = call(
            functools.partial(later_kernel, block, base, width),
            shape((rows, cols), BF),
            [SCALARS] + [WHOLE] * 15 + [ANYWHERE],
            ANYWHERE,
            info,
            src,
            kept,
            mine,
            put,
            *messages[k - 1],
            matrix,
            *panels,
            lower_inverse,
            upper_inverse,
            out,
            aliases={16: 0},
            scratch=[
                pltpu.VMEM((2 * block, span), BF),
                pltpu.VMEM((2 * block, span), BF),
                pltpu.VMEM((block, span), BF),
                pltpu.VMEM((block, span), BF),
                pltpu.SemaphoreType.DMA,
            ],
        )
    return out


def solution(mesh):
    placed = (P("row", "col"), P(), P(), P())
    return jax.shard_map(
        body, mesh=mesh, in_specs=placed, out_specs=P("row", "col"), check_vma=False
    )
```

```python
import functools

import jax
import jax.numpy as jnp
from jax import lax
from jax.experimental import pallas as pl
from jax.experimental.pallas import tpu as pltpu
from jax.sharding import PartitionSpec as P

BF = jnp.bfloat16
F32 = jnp.float32
I32 = jnp.int32
VMEM_LIMIT = 12 * 1024 * 1024
LANES = 128
ANYWHERE = pl.BlockSpec(memory_space=pl.ANY)
WHOLE = pl.BlockSpec(memory_space=pltpu.VMEM)
PARAMS = pltpu.CompilerParams(vmem_limit_bytes=VMEM_LIMIT)


def matmul(a, b):
    return jnp.dot(a, b, preferred_element_type=F32)


def rounded(a, b):
    return matmul(a, b).astype(BF)


def call(kernel, out_shape, in_specs, out_specs, *args, after=(), aliases=None, scratch=(), flops=1 << 27):
    moved = sum(a.size * a.dtype.itemsize for a in args)
    used = len(args)

    def ordered(*refs):
        kernel(*refs[:used], *refs[used + len(after) :])

    in_specs = list(in_specs) + [ANYWHERE] * len(after)
    args = args + tuple(after)
    return pl.pallas_call(
        ordered,
        grid=(1,),
        out_shape=out_shape,
        in_specs=in_specs,
        out_specs=out_specs,
        scratch_shapes=list(scratch),
        input_output_aliases=aliases or {},
        compiler_params=PARAMS,
        cost_estimate=pl.CostEstimate(flops=flops, bytes_accessed=moved, transcendentals=0),
    )(*args)


def pack_kernel(base, width, source, *outs):
    place = lax.rem(lax.axis_index("row"), 4)
    for d in range(4):
        start = pl.multiple_of(base + lax.bitwise_xor(place, d) * width, LANES)
        outs[d][...] = source[:, pl.ds(start, width)]


def pick(flags, values, axis):
    return jnp.sum(jnp.where(flags, values, 0.0), axis=axis, keepdims=True)


def found(flags, axis):
    return jnp.max(jnp.where(flags, 1.0, 0.0), axis=axis, keepdims=True) > 0.0


def plan_kernel(block, flat, src_out, foreign_out, kept_out, gather_out, displaced_out, mine_out, put_out):
    me = lax.axis_index("row")
    first_row = flat[0:1, :].astype(F32)
    second_row = flat[1:2, :].astype(F32)
    shape = (block, block)
    down = lax.broadcasted_iota(I32, shape, 0).astype(F32)
    along = lax.broadcasted_iota(I32, shape, 1).astype(F32)
    first_col = pick(down == along, first_row, 1)
    second_col = pick(down == along, second_row, 1)
    size = float(block)
    both = first_col == second_row
    both_turned = second_col == first_row
    inside = first_col == along + size
    inside_turned = first_row == down + size
    moved_row = jnp.where(found(inside, 0), pick(inside, down, 0), along[0:1] + size)
    moved_col = jnp.where(found(inside_turned, 1), pick(inside_turned, along, 1), down[:, 0:1] + size)
    source_row = jnp.where(found(both, 0), pick(both, down, 0), second_row)
    source_col = jnp.where(found(both_turned, 1), pick(both_turned, along, 1), second_col)
    shifted_col = jnp.where(found(both, 1), pick(both, moved_row, 1), down[:, 0:1])
    sources = jnp.concatenate([first_col, source_col], axis=0).astype(I32)
    displaced = jnp.concatenate([shifted_col, moved_col], axis=0).astype(I32)
    source_flat = jnp.concatenate([first_row, source_row], axis=1).astype(I32)
    src_out[...] = jnp.broadcast_to(sources, src_out.shape)
    square = me - lax.rem(me, 4)
    here = jnp.logical_and(sources >= square * block, sources < (square + 4) * block)
    leaves = sources >= 2 * block
    at_home = square == 0
    taken = jnp.where(here, sources, jnp.where(at_home, displaced, -1))
    gone = jnp.where(jnp.logical_and(leaves, at_home), displaced, -1)
    lanes = lax.broadcasted_iota(I32, (2 * block, block), 1)
    for d in range(4):
        cols = slice(d * block, (d + 1) * block)
        gather_out[:, cols] = jnp.where(taken - lax.bitwise_xor(me, d) * block == lanes, 1.0, 0.0).astype(BF)
    near = jnp.where(lax.rem(me, 4) < 2, 0, 2)
    for d in range(2):
        cols = slice(d * block, (d + 1) * block)
        base = lax.bitwise_xor(me, near + d) * block
        displaced_out[:, cols] = jnp.where(gone - base == lanes, 1.0, 0.0).astype(BF)
    mine_out[...] = jnp.where(sources - me * block == lanes, 1.0, 0.0).astype(BF)
    rows = lax.broadcasted_iota(I32, (block, 2 * block), 0) + me * block
    put = source_flat == rows
    put_out[...] = jnp.where(put, 1.0, 0.0).astype(BF)
    kept_out[...] = jnp.broadcast_to(jnp.where(found(put, 1), 0.0, 1.0), kept_out.shape).astype(BF)
    owned = jnp.logical_and(sources >= me * block, sources < (me + 1) * block)
    foreign_out[...] = jnp.broadcast_to(jnp.where(owned, 0.0, 1.0), foreign_out.shape).astype(BF)


def select_kernel(block, pieces, gather, displaced, *refs):
    count = pieces
    parts, rows = refs[: -2 * count - 1], refs[-1]
    kept, gone = refs[-2 * count - 1 : -count - 1], refs[-count - 1 : -1]
    start = 0
    for part in parts:
        rows[start : start + part.shape[0]] = part[...]
        start += part.shape[0]
    start = pl.multiple_of(jnp.where(lax.rem(lax.axis_index("row"), 4) < 2, 0, 2 * block), 2 * block)
    size = 2 * block // count
    for i in range(count):
        slots = slice(i * size, (i + 1) * size)
        kept[i][...] = rounded(gather[slots], rows[...])
        gone[i][...] = rounded(displaced[slots], rows[pl.ds(start, 2 * block)])


def tiles(width):
    return [slice(i, i + LANES) for i in range(0, width, LANES)]


def merge_kernel(block, last_side, pieces, src, *refs):
    kept, received, gone = refs[:pieces], refs[pieces : 2 * pieces], refs[2 * pieces : 3 * pieces]
    outs = refs[3 * pieces :]
    me = lax.axis_index("row")
    side = 4 * last_side
    mine = lax.div(me, side) * side * block
    low_side = me < side
    size = 2 * block // pieces
    for i in range(pieces):
        rows = slice(i * size, (i + 1) * size)
        sources = src[rows]
        from_here = jnp.logical_and(sources >= mine, sources < mine + side * block)
        leaves = sources >= 2 * block
        theirs = []
        for d in range(4):
            base = lax.bitwise_xor(me, d) * block
            theirs.append(jnp.logical_and(jnp.logical_and(sources >= base, sources < base + block), leaves))
        for cols in tiles(kept[i].shape[1]):
            arrived = received[i][:, cols].astype(F32)
            top = jnp.where(from_here, kept[i][:, cols].astype(F32), arrived)
            moved = jnp.where(low_side, gone[i][:, cols].astype(F32), arrived)
            for d in range(4):
                outs[d][rows, cols] = jnp.where(theirs[d], moved, top).astype(BF)


def assemble(block, base, width, me, foreign, kept, mine, put, messages, raw, slots, top, own):
    place = lax.rem(me, 4)
    span = 4 * width
    for d in range(4):
        start = pl.multiple_of(lax.bitwise_xor(place, d) * width, LANES)
        slots[:, pl.ds(start, width)] = messages[d][...]
    here = raw[:, base : base + span]
    candidates = rounded(mine[...], here)
    placed = rounded(put[...], slots[...])
    outside = foreign[...] > 0
    unmoved = kept[...] > 0
    for cols in tiles(span):
        top[:, cols] = jnp.where(outside, slots[:, cols], candidates[:, cols])
        own[:, cols] = jnp.where(unmoved, here[:, cols], placed[:, cols])

    @pl.when(me < 2)
    def _():
        own[...] = top[pl.ds(pl.multiple_of(me * block, block), block)]


def panel_kernel(block, base, width, foreign, kept, mine, put, m0, m1, m2, m3, raw, low, high, work, sent, more, slots):
    top, own = work.at[: 2 * block], work.at[2 * block :]
    assemble(block, base, width, lax.axis_index("row"), foreign, kept, mine, put, (m0, m1, m2, m3), raw, slots, top, own)

    @pl.when(lax.axis_index("col") == 0)
    def _():
        sent[...] = rounded(own[:, :block], high[0])
        more[...] = rounded(top[block:, :block], high[0])

    @pl.when(lax.axis_index("col") != 0)
    def _():
        sent[...] = own[:, :block]
        more[...] = rounded(low[0], top[:block, :block])


def finish(block, me, lower_own, lower_next, lower_second, low, top, own):
    upper = rounded(low[0], top[:block])
    following = (top[block:].astype(F32) - matmul(lower_next, upper)).astype(BF)
    upper_second = rounded(low[1], following)
    once = (own[...].astype(F32) - matmul(lower_own, upper)).astype(BF)
    twice = (once.astype(F32) - matmul(lower_second, upper_second)).astype(BF)
    return upper, following, jnp.where(me == 0, upper, jnp.where(me == 1, upper_second, twice))


def choose_kernel(reach, old, more, new, newer, *halves):
    my_col = lax.axis_index("col")
    fresh = jnp.logical_and(my_col >= reach, my_col < 2 * reach)
    half = halves[0].shape[0]
    for i, (stale, arrived) in enumerate(((old, new), (more, newer))):
        for j in range(2):
            rows = slice(j * half, (j + 1) * half)
            halves[2 * i + j][...] = jnp.where(fresh, arrived[rows], stale[rows])


def first_kernel(block, base, *refs):
    mine, theirs = refs[:4], refs[4:8]
    low, high, work, out, panels, result, done = refs[8:]
    even = lax.rem(lax.axis_index("col"), 2) == 0
    ours = [jnp.where(even, x[...], y[...]) for x, y in zip(mine, theirs)]
    rest = [jnp.where(even, y[...], x[...]) for x, y in zip(mine, theirs)]
    lower_own = jnp.concatenate(ours[:2])
    lower_next = jnp.concatenate(ours[2:])
    second_own = jnp.concatenate(rest[:2])
    head = jnp.concatenate(rest[2:])
    me = lax.axis_index("row")
    top, own = work.at[: 2 * block], work.at[2 * block :]
    panel = (second_own.astype(F32) - matmul(lower_own, head)).astype(BF)
    lower_second = rounded(panel, high[1])
    panels[:block] = lower_own
    panels[block : 2 * block] = lower_next
    panels[2 * block :] = lower_second
    upper, following, final = finish(block, me, lower_own, lower_next, lower_second, low, top, own)
    result[...] = final

    @pl.when(lax.axis_index("col") == 0)
    def _():
        result[:, :block] = jnp.where(me == 0, top[:block, :block], lower_own)

    @pl.when(lax.axis_index("col") == 1)
    def _():
        rest = jnp.where(me == 1, following[:, :block], lower_second)
        result[:, :block] = jnp.where(me == 0, upper[:, :block], rest)

    copy = pltpu.make_async_copy(result, out.at[:, pl.ds(base, result.shape[1])], done)
    copy.start()
    copy.wait()


def later_kernel(
    block, base, width, foreign, kept, mine, put, raw, panels, low, m0, m1, m2, m3,
    before, out, slots, top, own, result, done,
):
    me = lax.axis_index("row")
    assemble(block, base, width, me, foreign, kept, mine, put, (m0, m1, m2, m3), raw, slots, top, own)
    _, _, final = finish(block, me, panels[:block], panels[block : 2 * block], panels[2 * block :], low, top, own)
    result[...] = final
    copy = pltpu.make_async_copy(result, out.at[:, pl.ds(base, result.shape[1])], done)
    copy.start()
    copy.wait()


def exchange(value, bit, axis="row"):
    return lax.ppermute(value, axis, [(i, i ^ bit) for i in range(lax.axis_size(axis))])


def body(matrix, pivots, lower_inverse, upper_inverse):
    rows, cols = matrix.shape
    block = lower_inverse.shape[1]
    grid_rows = lax.axis_size("row")
    grid_cols = lax.axis_size("col")
    my_row = lax.axis_index("row")
    my_col = lax.axis_index("col")
    units = cols // (4 * LANES)
    widths = [1, units - 1]
    chunks = []
    base = 0
    for count in widths:
        chunks.append((base, count * LANES))
        base += 4 * count * LANES
    groups = grid_rows // 4
    last_side = max(groups // 2, 1)
    shape = jax.ShapeDtypeStruct

    def spread(chunk, after=()):
        mine, near, far, across = call(
            functools.partial(pack_kernel, *chunk),
            [shape((rows, chunk[1]), BF)] * 4,
            [WHOLE],
            [WHOLE] * 4,
            matrix,
            after=after,
        )
        return [mine, exchange(near, 1), exchange(far, 2), exchange(across, 3)]

    gathered = spread(chunks[0])

    src, foreign, kept, gather, displaced, mine, put = call(
        functools.partial(plan_kernel, block),
        [
            shape((2 * block, LANES), I32),
            shape((2 * block, LANES), BF),
            shape((block, LANES), BF),
            shape((2 * block, 4 * block), BF),
            shape((2 * block, 2 * block), BF),
            shape((2 * block, block), BF),
            shape((block, 2 * block), BF),
        ],
        [WHOLE],
        [WHOLE] * 7,
        pivots,
    )

    owner_group = src[:, :1] // block // 4
    my_group = my_row // 4

    def collect(part, width, pieces, after=()):
        size = 2 * block // pieces
        outs = call(
            functools.partial(select_kernel, block, pieces),
            [shape((size, width), BF)] * (2 * pieces),
            [WHOLE] * (2 + len(part)),
            [WHOLE] * (2 * pieces),
            gather,
            displaced,
            *part,
            after=after,
            scratch=[pltpu.VMEM((4 * block, width), BF)],
        )
        return outs[:pieces], outs[pieces:]

    def deliver(held, gone, width, after=()):
        pieces = len(held)
        side = 1
        while side < last_side:
            received = [exchange(piece, 4 * side) for piece in held]
            here = my_group // side
            owners = jnp.split(owner_group // side, pieces)
            keep = [jnp.logical_or(o == here, jnp.logical_and(here == 0, o != 1)) for o in owners]
            gone = [jnp.where(here == 1, new, old) for new, old in zip(received, gone)]
            held = [jnp.where(k, old, new) for k, old, new in zip(keep, held, received)]
            side *= 2
        received = [exchange(piece, 4 * side) for piece in held]
        messages = call(
            functools.partial(merge_kernel, block, last_side, pieces),
            [shape((2 * block, width), BF)] * 4,
            [WHOLE] * (1 + 3 * pieces),
            [WHOLE] * 4,
            src,
            *held,
            *received,
            *gone,
            after=after,
        )
        return [messages[0]] + [exchange(messages[d], d) for d in (1, 2, 3)]

    width = chunks[0][1]
    held, gone = collect(gathered, width, 1)
    collected = [collect(spread(chunk, after=[mine]), chunk[1], 2) for chunk in chunks[1:]]
    first = deliver(held, gone, width, after=[c[0][0] for c in collected])

    base, width = chunks[0]
    span = 4 * width
    work, *sent = call(
        functools.partial(panel_kernel, block, base, width),
        [shape((3 * block, span), BF)] + [shape((block, block), BF)] * 2,
        [WHOLE] * 11,
        [WHOLE] * 3,
        foreign,
        kept,
        mine,
        put,
        *first,
        matrix,
        lower_inverse,
        upper_inverse,
        scratch=[pltpu.VMEM((2 * block, span), BF)],
    )
    messages = [deliver(*c, width, after=sent[:1]) for c, (_, width) in zip(collected, chunks[1:])]
    reach = 2
    halves = [shape((block // 2, block), BF)] * 4
    while reach < grid_cols:
        arrived = [exchange(part, reach, "col") for part in sent]
        halved = call(functools.partial(choose_kernel, reach), halves, [WHOLE] * 4, [WHOLE] * 4, *sent, *arrived)
        reach *= 2
        if reach < grid_cols:
            sent = [jnp.concatenate(halved[:2]), jnp.concatenate(halved[2:])]
    other = [exchange(part, 1, "col") for part in halved]

    out, panels = call(
        functools.partial(first_kernel, block, base),
        [shape((rows, cols), BF), shape((3 * block, block), BF)],
        [WHOLE] * 11,
        [ANYWHERE, WHOLE],
        *halved,
        *other,
        lower_inverse,
        upper_inverse,
        work,
        scratch=[pltpu.VMEM((block, span), BF), pltpu.SemaphoreType.DMA],
    )
    for k in range(1, len(chunks)):
        base, width = chunks[k]
        span = 4 * width
        out = call(
            functools.partial(later_kernel, block, base, width),
            shape((rows, cols), BF),
            [WHOLE] * 11 + [ANYWHERE],
            ANYWHERE,
                foreign,
            kept,
            mine,
            put,
            matrix,
            panels,
            lower_inverse,
            *messages[k - 1],
            out,
            aliases={11: 0},
            scratch=[
                pltpu.VMEM((2 * block, span), BF),
                pltpu.VMEM((2 * block, span), BF),
                pltpu.VMEM((block, span), BF),
                pltpu.VMEM((block, span), BF),
                pltpu.SemaphoreType.DMA,
            ],
        )
    return out


def solution(mesh):
    placed = (P("row", "col"), P(), P(), P())
    return jax.shard_map(
        body, mesh=mesh, in_specs=placed, out_specs=P("row", "col"), check_vma=False
    )
```

```python
import functools

import jax
import jax.numpy as jnp
from jax import lax
from jax.experimental import pallas as pl
from jax.experimental.pallas import tpu as pltpu
from jax.sharding import PartitionSpec as P

BF = jnp.bfloat16
F32 = jnp.float32
I32 = jnp.int32
VMEM_LIMIT = 12 * 1024 * 1024
LANES = 128
ANYWHERE = pl.BlockSpec(memory_space=pl.ANY)
WHOLE = pl.BlockSpec(memory_space=pltpu.VMEM)
PARAMS = pltpu.CompilerParams(vmem_limit_bytes=VMEM_LIMIT)


def matmul(a, b):
    return jnp.dot(a, b, preferred_element_type=F32)


def rounded(a, b):
    return matmul(a, b).astype(BF)


def call(kernel, out_shape, in_specs, out_specs, *args, after=(), aliases=None, scratch=(), flops=1 << 27):
    moved = sum(a.size * a.dtype.itemsize for a in args)
    used = len(args)

    def ordered(*refs):
        kernel(*refs[:used], *refs[used + len(after) :])

    in_specs = list(in_specs) + [ANYWHERE] * len(after)
    args = args + tuple(after)
    return pl.pallas_call(
        ordered,
        grid=(1,),
        out_shape=out_shape,
        in_specs=in_specs,
        out_specs=out_specs,
        scratch_shapes=list(scratch),
        input_output_aliases=aliases or {},
        compiler_params=PARAMS,
        cost_estimate=pl.CostEstimate(flops=flops, bytes_accessed=moved, transcendentals=0),
    )(*args)


def pack_kernel(base, width, source, *outs):
    place = lax.rem(lax.axis_index("row"), 4)
    for d in range(4):
        start = pl.multiple_of(base + lax.bitwise_xor(place, d) * width, LANES)
        outs[d][...] = source[:, pl.ds(start, width)]


def pick(flags, values, axis):
    return jnp.sum(jnp.where(flags, values, 0.0), axis=axis, keepdims=True)


def found(flags, axis):
    return jnp.max(jnp.where(flags, 1.0, 0.0), axis=axis, keepdims=True) > 0.0


def plan_kernel(block, flat, src_out, foreign_out, kept_out, gather_out, displaced_out, mine_out, put_out):
    me = lax.axis_index("row")
    first_row = flat[0:1, :].astype(F32)
    second_row = flat[1:2, :].astype(F32)
    shape = (block, block)
    down = lax.broadcasted_iota(I32, shape, 0).astype(F32)
    along = lax.broadcasted_iota(I32, shape, 1).astype(F32)
    first_col = pick(down == along, first_row, 1)
    second_col = pick(down == along, second_row, 1)
    size = float(block)
    both = first_col == second_row
    both_turned = second_col == first_row
    inside = first_col == along + size
    inside_turned = first_row == down + size
    moved_row = jnp.where(found(inside, 0), pick(inside, down, 0), along[0:1] + size)
    moved_col = jnp.where(found(inside_turned, 1), pick(inside_turned, along, 1), down[:, 0:1] + size)
    source_row = jnp.where(found(both, 0), pick(both, down, 0), second_row)
    source_col = jnp.where(found(both_turned, 1), pick(both_turned, along, 1), second_col)
    shifted_col = jnp.where(found(both, 1), pick(both, moved_row, 1), down[:, 0:1])
    sources = jnp.concatenate([first_col, source_col], axis=0).astype(I32)
    displaced = jnp.concatenate([shifted_col, moved_col], axis=0).astype(I32)
    source_flat = jnp.concatenate([first_row, source_row], axis=1).astype(I32)
    src_out[...] = jnp.broadcast_to(sources, src_out.shape)
    square = me - lax.rem(me, 4)
    here = jnp.logical_and(sources >= square * block, sources < (square + 4) * block)
    leaves = sources >= 2 * block
    at_home = square == 0
    taken = jnp.where(here, sources, jnp.where(at_home, displaced, -1))
    gone = jnp.where(jnp.logical_and(leaves, at_home), displaced, -1)
    lanes = lax.broadcasted_iota(I32, (2 * block, block), 1)
    for d in range(4):
        cols = slice(d * block, (d + 1) * block)
        gather_out[:, cols] = jnp.where(taken - lax.bitwise_xor(me, d) * block == lanes, 1.0, 0.0).astype(BF)
    near = jnp.where(lax.rem(me, 4) < 2, 0, 2)
    for d in range(2):
        cols = slice(d * block, (d + 1) * block)
        base = lax.bitwise_xor(me, near + d) * block
        displaced_out[:, cols] = jnp.where(gone - base == lanes, 1.0, 0.0).astype(BF)
    mine_out[...] = jnp.where(sources - me * block == lanes, 1.0, 0.0).astype(BF)
    rows = lax.broadcasted_iota(I32, (block, 2 * block), 0) + me * block
    put = source_flat == rows
    put_out[...] = jnp.where(put, 1.0, 0.0).astype(BF)
    kept_out[...] = jnp.broadcast_to(jnp.where(found(put, 1), 0.0, 1.0), kept_out.shape).astype(BF)
    owned = jnp.logical_and(sources >= me * block, sources < (me + 1) * block)
    foreign_out[...] = jnp.broadcast_to(jnp.where(owned, 0.0, 1.0), foreign_out.shape).astype(BF)


def spans(sizes):
    return [slice(sum(sizes[:i]), sum(sizes[: i + 1])) for i in range(len(sizes))]


def select_kernel(block, pieces, gather, displaced, *refs):
    count = len(pieces)
    parts, rows = refs[: -2 * count - 1], refs[-1]
    kept, gone = refs[-2 * count - 1 : -count - 1], refs[-count - 1 : -1]
    start = 0
    for part in parts:
        rows[start : start + part.shape[0]] = part[...]
        start += part.shape[0]
    start = pl.multiple_of(jnp.where(lax.rem(lax.axis_index("row"), 4) < 2, 0, 2 * block), 2 * block)
    for i, slots in enumerate(spans(pieces)):
        kept[i][...] = rounded(gather[slots], rows[...])
        gone[i][...] = rounded(displaced[slots], rows[pl.ds(start, 2 * block)])


def tiles(width):
    return [slice(i, i + LANES) for i in range(0, width, LANES)]


def merge_kernel(block, last_side, pieces, src, *refs):
    count = len(pieces)
    kept, received, gone = refs[:count], refs[count : 2 * count], refs[2 * count : 3 * count]
    outs = refs[3 * count :]
    me = lax.axis_index("row")
    side = 4 * last_side
    mine = lax.div(me, side) * side * block
    low_side = me < side
    for i, rows in enumerate(spans(pieces)):
        sources = src[rows]
        from_here = jnp.logical_and(sources >= mine, sources < mine + side * block)
        leaves = sources >= 2 * block
        theirs = []
        for d in range(4):
            base = lax.bitwise_xor(me, d) * block
            theirs.append(jnp.logical_and(jnp.logical_and(sources >= base, sources < base + block), leaves))
        for cols in tiles(kept[i].shape[1]):
            arrived = received[i][:, cols].astype(F32)
            top = jnp.where(from_here, kept[i][:, cols].astype(F32), arrived)
            moved = jnp.where(low_side, gone[i][:, cols].astype(F32), arrived)
            for d in range(4):
                outs[d][rows, cols] = jnp.where(theirs[d], moved, top).astype(BF)


def settle(block, me, foreign, kept, mine, put, here, slots, top, own):
    candidates = rounded(mine[...], here)
    placed = rounded(put[...], slots[...])
    outside = foreign[...] > 0
    unmoved = kept[...] > 0
    for cols in tiles(here.shape[1]):
        top[:, cols] = jnp.where(outside, slots[:, cols], candidates[:, cols])
        own[:, cols] = jnp.where(unmoved, here[:, cols], placed[:, cols])

    @pl.when(me < 2)
    def _():
        own[...] = top[pl.ds(pl.multiple_of(me * block, block), block)]


def assemble(block, base, width, me, foreign, kept, mine, put, messages, raw, slots, top, own):
    place = lax.rem(me, 4)
    for d in range(4):
        start = pl.multiple_of(lax.bitwise_xor(place, d) * width, LANES)
        slots[:, pl.ds(start, width)] = messages[d][...]
    settle(block, me, foreign, kept, mine, put, raw[:, base : base + 4 * width], slots, top, own)


def panel_kernel(block, base, width, foreign, kept, mine, put, m0, m1, m2, m3, raw, low, high, work, sent, more, slots):
    top, own = work.at[: 2 * block], work.at[2 * block :]
    assemble(block, base, width, lax.axis_index("row"), foreign, kept, mine, put, (m0, m1, m2, m3), raw, slots, top, own)

    @pl.when(lax.axis_index("col") == 0)
    def _():
        sent[...] = rounded(own[:, :block], high[0])
        more[...] = rounded(top[block:, :block], high[0])

    @pl.when(lax.axis_index("col") != 0)
    def _():
        sent[...] = own[:, :block]
        more[...] = rounded(low[0], top[:block, :block])


def finish(block, me, lower_own, lower_next, lower_second, low, top, own):
    upper = rounded(low[0], top[:block])
    following = (top[block:].astype(F32) - matmul(lower_next, upper)).astype(BF)
    upper_second = rounded(low[1], following)
    once = (own[...].astype(F32) - matmul(lower_own, upper)).astype(BF)
    twice = (once.astype(F32) - matmul(lower_second, upper_second)).astype(BF)
    return upper, following, jnp.where(me == 0, upper, jnp.where(me == 1, upper_second, twice))


def choose_kernel(reach, old, more, new, newer, *halves):
    my_col = lax.axis_index("col")
    fresh = jnp.logical_and(my_col >= reach, my_col < 2 * reach)
    for out, stale, arrived in zip(halves, (old, more), (new, newer)):
        out[...] = jnp.where(fresh, arrived[...], stale[...])


def first_kernel(block, *refs):
    mine, theirs = refs[:2], refs[2:4]
    low, high, work, result, panels = refs[4:]
    even = lax.rem(lax.axis_index("col"), 2) == 0
    lower_own, lower_next = [jnp.where(even, x[...], y[...]) for x, y in zip(mine, theirs)]
    second_own, head = [jnp.where(even, y[...], x[...]) for x, y in zip(mine, theirs)]
    me = lax.axis_index("row")
    top, own = work.at[: 2 * block], work.at[2 * block :]
    panel = (second_own.astype(F32) - matmul(lower_own, head)).astype(BF)
    lower_second = rounded(panel, high[1])
    panels[:block] = lower_own
    panels[block : 2 * block] = lower_next
    panels[2 * block :] = lower_second
    upper, following, final = finish(block, me, lower_own, lower_next, lower_second, low, top, own)
    result[...] = final

    @pl.when(lax.axis_index("col") == 0)
    def _():
        result[:, :block] = jnp.where(me == 0, top[:block, :block], lower_own)

    @pl.when(lax.axis_index("col") == 1)
    def _():
        rest = jnp.where(me == 1, following[:, :block], lower_second)
        result[:, :block] = jnp.where(me == 0, upper[:, :block], rest)


def columns(base, width, quarters):
    place = lax.rem(lax.axis_index("row"), 4)
    return [pl.multiple_of(base + lax.bitwise_xor(place, d) * width, LANES) for d in quarters]


def sends(result, out, starts, width, done, first):
    copies = []
    for i, start in enumerate(starts):
        piece = result.at[:, pl.ds(i * width, width)]
        copies.append(pltpu.make_async_copy(piece, out.at[:, pl.ds(start, width)], done.at[first + i]))
        copies[i].start()
    return copies


def later_kernel(block, last, chunk, quarters, earlier, foreign, kept, mine, put, raw, panels, low, ready, *refs):
    count = len(quarters)
    messages = refs[:count]
    out, *result, rows, slots, top, own, done = refs[count + (earlier is not None) :]
    result = result[0]
    base, width = chunk
    me = lax.axis_index("row")
    if earlier is None:
        copies = sends(ready, out, [0], ready.shape[1], done, 0)
    else:
        copies = sends(ready, out, columns(*earlier), earlier[1], done, 0)
    starts = columns(base, width, quarters)
    for i, start in enumerate(starts):
        rows[:, i * width : (i + 1) * width] = raw[:, pl.ds(start, width)]
        slots[:, i * width : (i + 1) * width] = messages[i][...]
    settle(block, me, foreign, kept, mine, put, rows[...], slots, top, own)
    _, _, final = finish(block, me, panels[:block], panels[block : 2 * block], panels[2 * block :], low, top, own)
    result[...] = final
    if last:
        copies += sends(result, out, starts, width, done, len(copies))
    for copy in copies:
        copy.wait()


def exchange(value, bit, axis="row"):
    return lax.ppermute(value, axis, [(i, i ^ bit) for i in range(lax.axis_size(axis))])


def body(matrix, pivots, lower_inverse, upper_inverse):
    rows, cols = matrix.shape
    block = lower_inverse.shape[1]
    grid_rows = lax.axis_size("row")
    grid_cols = lax.axis_size("col")
    my_row = lax.axis_index("row")
    my_col = lax.axis_index("col")
    units = cols // (4 * LANES)
    widths = [1, units - 1]
    chunks = []
    base = 0
    for count in widths:
        chunks.append((base, count * LANES))
        base += 4 * count * LANES
    groups = grid_rows // 4
    last_side = max(groups // 2, 1)
    shape = jax.ShapeDtypeStruct

    def spread(chunk, after=()):
        mine, near, far, across = call(
            functools.partial(pack_kernel, *chunk),
            [shape((rows, chunk[1]), BF)] * 4,
            [WHOLE],
            [WHOLE] * 4,
            matrix,
            after=after,
        )
        return [mine, exchange(near, 1), exchange(far, 2), exchange(across, 3)]

    gathered = spread(chunks[0])

    src, foreign, kept, gather, displaced, mine, put = call(
        functools.partial(plan_kernel, block),
        [
            shape((2 * block, LANES), I32),
            shape((2 * block, LANES), BF),
            shape((block, LANES), BF),
            shape((2 * block, 4 * block), BF),
            shape((2 * block, 2 * block), BF),
            shape((2 * block, block), BF),
            shape((block, 2 * block), BF),
        ],
        [WHOLE],
        [WHOLE] * 7,
        pivots,
    )

    owner_group = src[:, :1] // block // 4
    my_group = my_row // 4

    def collect(part, width, pieces, after=()):
        count = len(pieces)
        slots = [shape((size, width), BF) for size in pieces]
        outs = call(
            functools.partial(select_kernel, block, pieces),
            slots * 2,
            [WHOLE] * (2 + len(part)),
            [WHOLE] * (2 * count),
            gather,
            displaced,
            *part,
            after=after,
            scratch=[pltpu.VMEM((4 * block, width), BF)],
        )
        return outs[:count], outs[count:]

    def deliver(held, gone, width, after=()):
        pieces = [piece.shape[0] for piece in held]
        side = 1
        while side < last_side:
            received = [exchange(piece, 4 * side) for piece in held]
            here = my_group // side
            owners = [owner_group[rows] // side for rows in spans(pieces)]
            keep = [jnp.logical_or(o == here, jnp.logical_and(here == 0, o != 1)) for o in owners]
            gone = [jnp.where(here == 1, new, old) for new, old in zip(received, gone)]
            held = [jnp.where(k, old, new) for k, old, new in zip(keep, held, received)]
            side *= 2
        received = [exchange(piece, 4 * side) for piece in held]
        messages = call(
            functools.partial(merge_kernel, block, last_side, pieces),
            [shape((2 * block, width), BF)] * 4,
            [WHOLE] * (1 + 3 * len(pieces)),
            [WHOLE] * 4,
            src,
            *held,
            *received,
            *gone,
            after=after,
        )
        return [messages[0]] + [exchange(messages[d], d) for d in (1, 2, 3)]

    width = chunks[0][1]
    held, gone = collect(gathered, width, [2 * block])
    collected = [collect(spread(chunk, after=[mine]), chunk[1], [2 * block - 160, 160]) for chunk in chunks[1:]]
    first = deliver(held, gone, width, after=[c[0][0] for c in collected])

    base, width = chunks[0]
    span = 4 * width
    work, *sent = call(
        functools.partial(panel_kernel, block, base, width),
        [shape((3 * block, span), BF)] + [shape((block, block), BF)] * 2,
        [WHOLE] * 11,
        [WHOLE] * 3,
        foreign,
        kept,
        mine,
        put,
        *first,
        matrix,
        lower_inverse,
        upper_inverse,
        scratch=[pltpu.VMEM((2 * block, span), BF)],
    )
    messages = [deliver(*c, width, after=sent[:1]) for c, (_, width) in zip(collected, chunks[1:])]
    reach = 2
    halves = [shape((block, block), BF)] * 2
    while reach < grid_cols:
        arrived = [exchange(part, reach, "col") for part in sent]
        halved = call(functools.partial(choose_kernel, reach), halves, [WHOLE] * 4, [WHOLE] * 2, *sent, *arrived)
        reach *= 2
        if reach < grid_cols:
            sent = halved
    other = [exchange(part, 1, "col") for part in halved]

    ready, panels = call(
        functools.partial(first_kernel, block),
        [shape((block, span), BF), shape((3 * block, block), BF)],
        [WHOLE] * 7,
        [WHOLE, WHOLE],
        *halved,
        *other,
        lower_inverse,
        upper_inverse,
        work,
    )
    stages = [(k, quarters) for k in range(1, len(chunks)) for quarters in ((0, 1, 2), (3,))]
    earlier, out = None, []
    for index, (k, quarters) in enumerate(stages):
        last = index == len(stages) - 1
        count = len(quarters)
        base, width = chunks[k]
        span = count * width
        result = shape((block, span), BF)
        scratch = [
            pltpu.VMEM((block, span), BF),
            pltpu.VMEM((2 * block, span), BF),
            pltpu.VMEM((2 * block, span), BF),
            pltpu.VMEM((block, span), BF),
            pltpu.SemaphoreType.DMA((8,)),
        ]
        out, *results = call(
            functools.partial(later_kernel, block, last, chunks[k], quarters, earlier),
            [shape((rows, cols), BF)] + [result] * (not last),
            [WHOLE] * (8 + count) + [ANYWHERE] * len(out),
            [ANYWHERE] + [WHOLE] * (not last),
            foreign,
            kept,
            mine,
            put,
            matrix,
            panels,
            lower_inverse,
            ready,
            *[messages[k - 1][d] for d in quarters],
            *out,
            aliases={8 + count: 0} if out else {},
            scratch=[pltpu.VMEM((block, span), BF)] * last + scratch,
        )
        earlier = (base, width, quarters)
        ready, out = (results or [None])[0], [out]
    return out[0]


def solution(mesh):
    placed = (P("row", "col"), P(), P(), P())
    return jax.shard_map(
        body, mesh=mesh, in_specs=placed, out_specs=P("row", "col"), check_vma=False
    )
```

```python
import functools

import jax
import jax.numpy as jnp
from jax import lax
from jax.experimental import pallas as pl
from jax.experimental.pallas import tpu as pltpu
from jax.sharding import PartitionSpec as P

BF = jnp.bfloat16
F32 = jnp.float32
I32 = jnp.int32
VMEM_LIMIT = 12 * 1024 * 1024
LANES = 128
ANYWHERE = pl.BlockSpec(memory_space=pl.ANY)
WHOLE = pl.BlockSpec(memory_space=pltpu.VMEM)
PARAMS = pltpu.CompilerParams(vmem_limit_bytes=VMEM_LIMIT)


def matmul(a, b):
    return jnp.dot(a, b, preferred_element_type=F32)


def rounded(a, b):
    return matmul(a, b).astype(BF)


def call(kernel, out_shape, in_specs, out_specs, *args, after=(), aliases=None, scratch=(), flops=1 << 27):
    moved = sum(a.size * a.dtype.itemsize for a in args)
    used = len(args)

    def ordered(*refs):
        kernel(*refs[:used], *refs[used + len(after) :])

    in_specs = list(in_specs) + [ANYWHERE] * len(after)
    args = args + tuple(after)
    return pl.pallas_call(
        ordered,
        grid=(1,),
        out_shape=out_shape,
        in_specs=in_specs,
        out_specs=out_specs,
        scratch_shapes=list(scratch),
        input_output_aliases=aliases or {},
        compiler_params=PARAMS,
        cost_estimate=pl.CostEstimate(flops=flops, bytes_accessed=moved, transcendentals=0),
    )(*args)


def pack_kernel(base, width, source, *outs):
    place = lax.rem(lax.axis_index("row"), 4)
    for d in range(4):
        start = pl.multiple_of(base + lax.bitwise_xor(place, d) * width, LANES)
        outs[d][...] = source[:, pl.ds(start, width)]


def pick(flags, values, axis):
    return jnp.sum(jnp.where(flags, values, 0.0), axis=axis, keepdims=True)


def found(flags, axis):
    return jnp.max(jnp.where(flags, 1.0, 0.0), axis=axis, keepdims=True) > 0.0


def plan_kernel(block, flat, src_out, foreign_out, kept_out, gather_out, displaced_out, mine_out, put_out):
    me = lax.axis_index("row")
    first_row = flat[0:1, :].astype(F32)
    second_row = flat[1:2, :].astype(F32)
    shape = (block, block)
    down = lax.broadcasted_iota(I32, shape, 0).astype(F32)
    along = lax.broadcasted_iota(I32, shape, 1).astype(F32)
    first_col = pick(down == along, first_row, 1)
    second_col = pick(down == along, second_row, 1)
    size = float(block)
    both = first_col == second_row
    both_turned = second_col == first_row
    inside = first_col == along + size
    inside_turned = first_row == down + size
    moved_row = jnp.where(found(inside, 0), pick(inside, down, 0), along[0:1] + size)
    moved_col = jnp.where(found(inside_turned, 1), pick(inside_turned, along, 1), down[:, 0:1] + size)
    source_row = jnp.where(found(both, 0), pick(both, down, 0), second_row)
    source_col = jnp.where(found(both_turned, 1), pick(both_turned, along, 1), second_col)
    shifted_col = jnp.where(found(both, 1), pick(both, moved_row, 1), down[:, 0:1])
    sources = jnp.concatenate([first_col, source_col], axis=0).astype(I32)
    displaced = jnp.concatenate([shifted_col, moved_col], axis=0).astype(I32)
    source_flat = jnp.concatenate([first_row, source_row], axis=1).astype(I32)
    src_out[...] = jnp.broadcast_to(sources, src_out.shape)
    square = me - lax.rem(me, 4)
    here = jnp.logical_and(sources >= square * block, sources < (square + 4) * block)
    leaves = sources >= 2 * block
    at_home = square == 0
    taken = jnp.where(here, sources, jnp.where(at_home, displaced, -1))
    gone = jnp.where(jnp.logical_and(leaves, at_home), displaced, -1)
    lanes = lax.broadcasted_iota(I32, (2 * block, block), 1)
    for d in range(4):
        cols = slice(d * block, (d + 1) * block)
        gather_out[:, cols] = jnp.where(taken - lax.bitwise_xor(me, d) * block == lanes, 1.0, 0.0).astype(BF)
    near = jnp.where(lax.rem(me, 4) < 2, 0, 2)
    for d in range(2):
        cols = slice(d * block, (d + 1) * block)
        base = lax.bitwise_xor(me, near + d) * block
        displaced_out[:, cols] = jnp.where(gone - base == lanes, 1.0, 0.0).astype(BF)
    mine_out[...] = jnp.where(sources - me * block == lanes, 1.0, 0.0).astype(BF)
    rows = lax.broadcasted_iota(I32, (block, 2 * block), 0) + me * block
    put = source_flat == rows
    put_out[...] = jnp.where(put, 1.0, 0.0).astype(BF)
    kept_out[...] = jnp.broadcast_to(jnp.where(found(put, 1), 0.0, 1.0), kept_out.shape).astype(BF)
    owned = jnp.logical_and(sources >= me * block, sources < (me + 1) * block)
    foreign_out[...] = jnp.broadcast_to(jnp.where(owned, 0.0, 1.0), foreign_out.shape).astype(BF)


def spans(sizes):
    return [slice(sum(sizes[:i]), sum(sizes[: i + 1])) for i in range(len(sizes))]


def select_kernel(block, pieces, gather, displaced, *refs):
    count = len(pieces)
    parts, rows = refs[: -2 * count - 1], refs[-1]
    kept, gone = refs[-2 * count - 1 : -count - 1], refs[-count - 1 : -1]
    start = 0
    for part in parts:
        rows[start : start + part.shape[0]] = part[...]
        start += part.shape[0]
    start = pl.multiple_of(jnp.where(lax.rem(lax.axis_index("row"), 4) < 2, 0, 2 * block), 2 * block)
    for i, slots in enumerate(spans(pieces)):
        kept[i][...] = rounded(gather[slots], rows[...])
        gone[i][...] = rounded(displaced[slots], rows[pl.ds(start, 2 * block)])


def tiles(width):
    return [slice(i, i + LANES) for i in range(0, width, LANES)]


def merge_kernel(block, last_side, pieces, src, *refs):
    count = len(pieces)
    kept, received, gone = refs[:count], refs[count : 2 * count], refs[2 * count : 3 * count]
    outs = refs[3 * count :]
    me = lax.axis_index("row")
    side = 4 * last_side
    mine = lax.div(me, side) * side * block
    low_side = me < side
    for i, rows in enumerate(spans(pieces)):
        sources = src[rows]
        from_here = jnp.logical_and(sources >= mine, sources < mine + side * block)
        leaves = sources >= 2 * block
        theirs = []
        for d in range(4):
            base = lax.bitwise_xor(me, d) * block
            theirs.append(jnp.logical_and(jnp.logical_and(sources >= base, sources < base + block), leaves))
        for cols in tiles(kept[i].shape[1]):
            arrived = received[i][:, cols].astype(F32)
            top = jnp.where(from_here, kept[i][:, cols].astype(F32), arrived)
            moved = jnp.where(low_side, gone[i][:, cols].astype(F32), arrived)
            for d in range(4):
                outs[d][rows, cols] = jnp.where(theirs[d], moved, top).astype(BF)


def settle(block, me, foreign, kept, mine, put, here, slots, top, own):
    candidates = rounded(mine[...], here)
    placed = rounded(put[...], slots[...])
    outside = foreign[...] > 0
    unmoved = kept[...] > 0
    for cols in tiles(here.shape[1]):
        top[:, cols] = jnp.where(outside, slots[:, cols], candidates[:, cols])
        own[:, cols] = jnp.where(unmoved, here[:, cols], placed[:, cols])

    @pl.when(me < 2)
    def _():
        own[...] = top[pl.ds(pl.multiple_of(jnp.minimum(me, 1) * block, block), block)]


def assemble(block, base, width, me, foreign, kept, mine, put, messages, raw, slots, top, own):
    place = lax.rem(me, 4)
    for d in range(4):
        start = pl.multiple_of(lax.bitwise_xor(place, d) * width, LANES)
        slots[:, pl.ds(start, width)] = messages[d][...]
    settle(block, me, foreign, kept, mine, put, raw[:, base : base + 4 * width], slots, top, own)


def panel_kernel(block, base, width, foreign, kept, mine, put, m0, m1, m2, m3, raw, low, high, work, sent, more, slots):
    top, own = work.at[: 2 * block], work.at[2 * block :]
    assemble(block, base, width, lax.axis_index("row"), foreign, kept, mine, put, (m0, m1, m2, m3), raw, slots, top, own)

    @pl.when(lax.axis_index("col") == 0)
    def _():
        sent[...] = rounded(own[:, :block], high[0])
        more[...] = rounded(top[block:, :block], high[0])

    @pl.when(lax.axis_index("col") != 0)
    def _():
        sent[...] = own[:, :block]
        more[...] = rounded(low[0], top[:block, :block])


def finish(block, me, lower_own, lower_next, lower_second, low, top, own):
    upper = rounded(low[0], top[:block])
    following = (top[block:].astype(F32) - matmul(lower_next, upper)).astype(BF)
    upper_second = rounded(low[1], following)
    once = (own[...].astype(F32) - matmul(lower_own, upper)).astype(BF)
    twice = (once.astype(F32) - matmul(lower_second, upper_second)).astype(BF)
    return upper, following, jnp.where(me == 0, upper, jnp.where(me == 1, upper_second, twice))


def choose_kernel(reach, old, more, new, newer, *halves):
    my_col = lax.axis_index("col")
    fresh = jnp.logical_and(my_col >= reach, my_col < 2 * reach)
    for out, stale, arrived in zip(halves, (old, more), (new, newer)):
        out[...] = jnp.where(fresh, arrived[...], stale[...])


def first_kernel(block, *refs):
    mine, theirs = refs[:2], refs[2:4]
    low, high, work, result, panels = refs[4:]
    even = lax.rem(lax.axis_index("col"), 2) == 0
    lower_own, lower_next = [jnp.where(even, x[...], y[...]) for x, y in zip(mine, theirs)]
    second_own, head = [jnp.where(even, y[...], x[...]) for x, y in zip(mine, theirs)]
    me = lax.axis_index("row")
    top, own = work.at[: 2 * block], work.at[2 * block :]
    panel = (second_own.astype(F32) - matmul(lower_own, head)).astype(BF)
    lower_second = rounded(panel, high[1])
    panels[:block] = lower_own
    panels[block : 2 * block] = lower_next
    panels[2 * block :] = lower_second
    upper, following, final = finish(block, me, lower_own, lower_next, lower_second, low, top, own)
    result[...] = final

    @pl.when(lax.axis_index("col") == 0)
    def _():
        result[:, :block] = jnp.where(me == 0, top[:block, :block], lower_own)

    @pl.when(lax.axis_index("col") == 1)
    def _():
        rest = jnp.where(me == 1, following[:, :block], lower_second)
        result[:, :block] = jnp.where(me == 0, upper[:, :block], rest)


def columns(base, width, quarters):
    place = lax.rem(lax.axis_index("row"), 4)
    return [pl.multiple_of(base + lax.bitwise_xor(place, d) * width, LANES) for d in quarters]


def sends(result, out, starts, width, done, first):
    copies = []
    for i, start in enumerate(starts):
        piece = result.at[:, pl.ds(i * width, width)]
        copies.append(pltpu.make_async_copy(piece, out.at[:, pl.ds(start, width)], done.at[first + i]))
        copies[i].start()
    return copies


def later_kernel(block, last, chunk, quarters, earlier, foreign, kept, mine, put, raw, panels, low, ready, *refs):
    count = len(quarters)
    messages = refs[:count]
    out, *result, rows, slots, top, own, done = refs[count + (earlier is not None) :]
    result = result[0]
    base, width = chunk
    me = lax.axis_index("row")
    if earlier is None:
        copies = sends(ready, out, [0], ready.shape[1], done, 0)
    else:
        copies = sends(ready, out, columns(*earlier), earlier[1], done, 0)
    starts = columns(base, width, quarters)
    for i, start in enumerate(starts):
        rows[:, i * width : (i + 1) * width] = raw[:, pl.ds(start, width)]
        slots[:, i * width : (i + 1) * width] = messages[i][...]
    settle(block, me, foreign, kept, mine, put, rows[...], slots, top, own)
    _, _, final = finish(block, me, panels[:block], panels[block : 2 * block], panels[2 * block :], low, top, own)
    result[...] = final
    if last:
        copies += sends(result, out, starts, width, done, len(copies))
    for copy in copies:
        copy.wait()


def exchange(value, bit, axis="row"):
    return lax.ppermute(value, axis, [(i, i ^ bit) for i in range(lax.axis_size(axis))])


def body(matrix, pivots, lower_inverse, upper_inverse):
    rows, cols = matrix.shape
    block = lower_inverse.shape[1]
    grid_rows = lax.axis_size("row")
    grid_cols = lax.axis_size("col")
    my_row = lax.axis_index("row")
    my_col = lax.axis_index("col")
    units = cols // (4 * LANES)
    widths = [1, units - 1]
    chunks = []
    base = 0
    for count in widths:
        chunks.append((base, count * LANES))
        base += 4 * count * LANES
    groups = grid_rows // 4
    last_side = max(groups // 2, 1)
    shape = jax.ShapeDtypeStruct

    def spread(chunk, after=()):
        mine, near, far, across = call(
            functools.partial(pack_kernel, *chunk),
            [shape((rows, chunk[1]), BF)] * 4,
            [WHOLE],
            [WHOLE] * 4,
            matrix,
            after=after,
        )
        return [mine, exchange(near, 1), exchange(far, 2), exchange(across, 3)]

    gathered = spread(chunks[0])

    src, foreign, kept, gather, displaced, mine, put = call(
        functools.partial(plan_kernel, block),
        [
            shape((2 * block, LANES), I32),
            shape((2 * block, LANES), BF),
            shape((block, LANES), BF),
            shape((2 * block, 4 * block), BF),
            shape((2 * block, 2 * block), BF),
            shape((2 * block, block), BF),
            shape((block, 2 * block), BF),
        ],
        [WHOLE],
        [WHOLE] * 7,
        pivots,
    )

    owner_group = src[:, :1] // block // 4
    my_group = my_row // 4

    def collect(part, width, pieces, after=()):
        count = len(pieces)
        slots = [shape((size, width), BF) for size in pieces]
        outs = call(
            functools.partial(select_kernel, block, pieces),
            slots * 2,
            [WHOLE] * (2 + len(part)),
            [WHOLE] * (2 * count),
            gather,
            displaced,
            *part,
            after=after,
            scratch=[pltpu.VMEM((4 * block, width), BF)],
        )
        return outs[:count], outs[count:]

    def deliver(held, gone, width, after=()):
        pieces = [piece.shape[0] for piece in held]
        side = 1
        while side < last_side:
            received = [exchange(piece, 4 * side) for piece in held]
            here = my_group // side
            owners = [owner_group[rows] // side for rows in spans(pieces)]
            keep = [jnp.logical_or(o == here, jnp.logical_and(here == 0, o != 1)) for o in owners]
            gone = [jnp.where(here == 1, new, old) for new, old in zip(received, gone)]
            held = [jnp.where(k, old, new) for k, old, new in zip(keep, held, received)]
            side *= 2
        received = [exchange(piece, 4 * side) for piece in held]
        messages = call(
            functools.partial(merge_kernel, block, last_side, pieces),
            [shape((2 * block, width), BF)] * 4,
            [WHOLE] * (1 + 3 * len(pieces)),
            [WHOLE] * 4,
            src,
            *held,
            *received,
            *gone,
            after=after,
        )
        return [messages[0]] + [exchange(messages[d], d) for d in (1, 2, 3)]

    width = chunks[0][1]
    held, gone = collect(gathered, width, [2 * block])
    collected = [collect(spread(chunk, after=[mine]), chunk[1], [2 * block - 160, 160]) for chunk in chunks[1:]]
    first = deliver(held, gone, width, after=[c[0][0] for c in collected])

    base, width = chunks[0]
    span = 4 * width
    work, *sent = call(
        functools.partial(panel_kernel, block, base, width),
        [shape((3 * block, span), BF)] + [shape((block, block), BF)] * 2,
        [WHOLE] * 11,
        [WHOLE] * 3,
        foreign,
        kept,
        mine,
        put,
        *first,
        matrix,
        lower_inverse,
        upper_inverse,
        scratch=[pltpu.VMEM((2 * block, span), BF)],
    )
    messages = [deliver(*c, width, after=sent[:1]) for c, (_, width) in zip(collected, chunks[1:])]
    reach = 2
    halved = sent
    halves = [shape((block, block), BF)] * 2
    while reach < grid_cols:
        arrived = [exchange(part, reach, "col") for part in sent]
        halved = call(functools.partial(choose_kernel, reach), halves, [WHOLE] * 4, [WHOLE] * 2, *sent, *arrived)
        reach *= 2
        if reach < grid_cols:
            sent = halved
    other = [exchange(part, 1, "col") for part in halved]

    ready, panels = call(
        functools.partial(first_kernel, block),
        [shape((block, span), BF), shape((3 * block, block), BF)],
        [WHOLE] * 7,
        [WHOLE, WHOLE],
        *halved,
        *other,
        lower_inverse,
        upper_inverse,
        work,
    )
    stages = [(k, quarters) for k in range(1, len(chunks)) for quarters in ((0, 1, 2), (3,))]
    earlier, out = None, []
    for index, (k, quarters) in enumerate(stages):
        last = index == len(stages) - 1
        count = len(quarters)
        base, width = chunks[k]
        span = count * width
        result = shape((block, span), BF)
        scratch = [
            pltpu.VMEM((block, span), BF),
            pltpu.VMEM((2 * block, span), BF),
            pltpu.VMEM((2 * block, span), BF),
            pltpu.VMEM((block, span), BF),
            pltpu.SemaphoreType.DMA((8,)),
        ]
        out, *results = call(
            functools.partial(later_kernel, block, last, chunks[k], quarters, earlier),
            [shape((rows, cols), BF)] + [result] * (not last),
            [WHOLE] * (8 + count) + [ANYWHERE] * len(out),
            [ANYWHERE] + [WHOLE] * (not last),
            foreign,
            kept,
            mine,
            put,
            matrix,
            panels,
            lower_inverse,
            ready,
            *[messages[k - 1][d] for d in quarters],
            *out,
            aliases={8 + count: 0} if out else {},
            scratch=[pltpu.VMEM((block, span), BF)] * last + scratch,
        )
        earlier = (base, width, quarters)
        ready, out = (results or [None])[0], [out]
    return out[0]


def solution(mesh):
    placed = (P("row", "col"), P(), P(), P())
    return jax.shard_map(
        body, mesh=mesh, in_specs=placed, out_specs=P("row", "col"), check_vma=False
    )
```

```python
import functools

import jax
import jax.numpy as jnp
from jax import lax
from jax.experimental import pallas as pl
from jax.experimental.pallas import tpu as pltpu
from jax.sharding import PartitionSpec as P

BF = jnp.bfloat16
F32 = jnp.float32
I32 = jnp.int32
VMEM_LIMIT = 12 * 1024 * 1024
LANES = 128
ANYWHERE = pl.BlockSpec(memory_space=pl.ANY)
WHOLE = pl.BlockSpec(memory_space=pltpu.VMEM)
PARAMS = pltpu.CompilerParams(vmem_limit_bytes=VMEM_LIMIT)


def matmul(a, b):
    return jnp.dot(a, b, preferred_element_type=F32)


def rounded(a, b):
    return matmul(a, b).astype(BF)


def call(kernel, out_shape, in_specs, out_specs, *args, after=(), aliases=None, scratch=(), flops=1 << 27):
    moved = sum(a.size * a.dtype.itemsize for a in args)
    used = len(args)

    def ordered(*refs):
        kernel(*refs[:used], *refs[used + len(after) :])

    in_specs = list(in_specs) + [ANYWHERE] * len(after)
    args = args + tuple(after)
    return pl.pallas_call(
        ordered,
        grid=(1,),
        out_shape=out_shape,
        in_specs=in_specs,
        out_specs=out_specs,
        scratch_shapes=list(scratch),
        input_output_aliases=aliases or {},
        compiler_params=PARAMS,
        cost_estimate=pl.CostEstimate(flops=flops, bytes_accessed=moved, transcendentals=0),
    )(*args)


def pack_kernel(base, width, source, *outs):
    place = lax.rem(lax.axis_index("row"), 4)
    for d in range(4):
        start = pl.multiple_of(base + lax.bitwise_xor(place, d) * width, LANES)
        outs[d][...] = source[:, pl.ds(start, width)]


def pick(flags, values, axis):
    return jnp.sum(jnp.where(flags, values, 0.0), axis=axis, keepdims=True)


def found(flags, axis):
    return jnp.max(jnp.where(flags, 1.0, 0.0), axis=axis, keepdims=True) > 0.0


def plan_kernel(block, flat, src_out, foreign_out, kept_out, gather_out, displaced_out, mine_out, put_out):
    me = lax.axis_index("row")
    first_row = flat[0:1, :].astype(F32)
    second_row = flat[1:2, :].astype(F32)
    shape = (block, block)
    down = lax.broadcasted_iota(I32, shape, 0).astype(F32)
    along = lax.broadcasted_iota(I32, shape, 1).astype(F32)
    first_col = pick(down == along, first_row, 1)
    second_col = pick(down == along, second_row, 1)
    size = float(block)
    both = first_col == second_row
    both_turned = second_col == first_row
    inside = first_col == along + size
    inside_turned = first_row == down + size
    moved_row = jnp.where(found(inside, 0), pick(inside, down, 0), along[0:1] + size)
    moved_col = jnp.where(found(inside_turned, 1), pick(inside_turned, along, 1), down[:, 0:1] + size)
    source_row = jnp.where(found(both, 0), pick(both, down, 0), second_row)
    source_col = jnp.where(found(both_turned, 1), pick(both_turned, along, 1), second_col)
    shifted_col = jnp.where(found(both, 1), pick(both, moved_row, 1), down[:, 0:1])
    sources = jnp.concatenate([first_col, source_col], axis=0).astype(I32)
    displaced = jnp.concatenate([shifted_col, moved_col], axis=0).astype(I32)
    source_flat = jnp.concatenate([first_row, source_row], axis=1).astype(I32)
    src_out[...] = jnp.broadcast_to(sources, src_out.shape)
    square = me - lax.rem(me, 4)
    here = jnp.logical_and(sources >= square * block, sources < (square + 4) * block)
    leaves = sources >= 2 * block
    at_home = square == 0
    taken = jnp.where(here, sources, jnp.where(at_home, displaced, -1))
    gone = jnp.where(jnp.logical_and(leaves, at_home), displaced, -1)
    lanes = lax.broadcasted_iota(I32, (2 * block, block), 1)
    for d in range(4):
        cols = slice(d * block, (d + 1) * block)
        gather_out[:, cols] = jnp.where(taken - lax.bitwise_xor(me, d) * block == lanes, 1.0, 0.0).astype(BF)
    near = jnp.where(lax.rem(me, 4) < 2, 0, 2)
    for d in range(2):
        cols = slice(d * block, (d + 1) * block)
        base = lax.bitwise_xor(me, near + d) * block
        displaced_out[:, cols] = jnp.where(gone - base == lanes, 1.0, 0.0).astype(BF)
    mine_out[...] = jnp.where(sources - me * block == lanes, 1.0, 0.0).astype(BF)
    rows = lax.broadcasted_iota(I32, (block, 2 * block), 0) + me * block
    put = source_flat == rows
    put_out[...] = jnp.where(put, 1.0, 0.0).astype(BF)
    kept_out[...] = jnp.broadcast_to(jnp.where(found(put, 1), 0.0, 1.0), kept_out.shape).astype(BF)
    owned = jnp.logical_and(sources >= me * block, sources < (me + 1) * block)
    foreign_out[...] = jnp.broadcast_to(jnp.where(owned, 0.0, 1.0), foreign_out.shape).astype(BF)


def spans(sizes):
    return [slice(sum(sizes[:i]), sum(sizes[: i + 1])) for i in range(len(sizes))]


def select_kernel(block, pieces, gather, displaced, *refs):
    count = len(pieces)
    parts, rows = refs[: -2 * count - 1], refs[-1]
    kept, gone = refs[-2 * count - 1 : -count - 1], refs[-count - 1 : -1]
    start = 0
    for part in parts:
        rows[start : start + part.shape[0]] = part[...]
        start += part.shape[0]
    start = pl.multiple_of(jnp.where(lax.rem(lax.axis_index("row"), 4) < 2, 0, 2 * block), 2 * block)
    for i, slots in enumerate(spans(pieces)):
        kept[i][...] = rounded(gather[slots], rows[...])
        gone[i][...] = rounded(displaced[slots], rows[pl.ds(start, 2 * block)])


def tiles(width):
    return [slice(i, i + LANES) for i in range(0, width, LANES)]


def merge_kernel(block, last_side, pieces, src, *refs):
    count = len(pieces)
    kept, received, gone = refs[:count], refs[count : 2 * count], refs[2 * count : 3 * count]
    outs = refs[3 * count :]
    me = lax.axis_index("row")
    side = 4 * last_side
    mine = lax.div(me, side) * side * block
    low_side = me < side
    for i, rows in enumerate(spans(pieces)):
        sources = src[rows]
        from_here = jnp.logical_and(sources >= mine, sources < mine + side * block)
        leaves = sources >= 2 * block
        theirs = []
        for d in range(4):
            base = lax.bitwise_xor(me, d) * block
            theirs.append(jnp.logical_and(jnp.logical_and(sources >= base, sources < base + block), leaves))
        for cols in tiles(kept[i].shape[1]):
            arrived = received[i][:, cols].astype(F32)
            top = jnp.where(from_here, kept[i][:, cols].astype(F32), arrived)
            moved = jnp.where(low_side, gone[i][:, cols].astype(F32), arrived)
            for d in range(4):
                outs[d][rows, cols] = jnp.where(theirs[d], moved, top).astype(BF)


def settle(block, me, foreign, kept, mine, put, here, slots, top, own):
    candidates = rounded(mine[...], here)
    placed = rounded(put[...], slots[...])
    outside = foreign[...] > 0
    unmoved = kept[...] > 0
    for cols in tiles(here.shape[1]):
        top[:, cols] = jnp.where(outside, slots[:, cols], candidates[:, cols])
        own[:, cols] = jnp.where(unmoved, here[:, cols], placed[:, cols])

    @pl.when(me < 2)
    def _():
        own[...] = top[pl.ds(pl.multiple_of(jnp.minimum(me, 1) * block, block), block)]


def assemble(block, base, width, me, foreign, kept, mine, put, messages, raw, slots, top, own):
    place = lax.rem(me, 4)
    for d in range(4):
        start = pl.multiple_of(lax.bitwise_xor(place, d) * width, LANES)
        slots[:, pl.ds(start, width)] = messages[d][...]
    settle(block, me, foreign, kept, mine, put, raw[:, base : base + 4 * width], slots, top, own)


def panel_kernel(block, base, width, foreign, kept, mine, put, m0, m1, m2, m3, raw, low, high, work, sent, more, slots):
    top, own = work.at[: 2 * block], work.at[2 * block :]
    assemble(block, base, width, lax.axis_index("row"), foreign, kept, mine, put, (m0, m1, m2, m3), raw, slots, top, own)

    @pl.when(lax.axis_index("col") == 0)
    def _():
        sent[...] = rounded(own[:, :block], high[0])
        more[...] = rounded(top[block:, :block], high[0])

    @pl.when(lax.axis_index("col") != 0)
    def _():
        sent[...] = own[:, :block]
        more[...] = rounded(low[0], top[:block, :block])


def finish(block, me, lower_own, lower_next, lower_second, low, top, own):
    upper = rounded(low[0], top[:block])
    following = (top[block:].astype(F32) - matmul(lower_next, upper)).astype(BF)
    upper_second = rounded(low[1], following)
    once = (own[...].astype(F32) - matmul(lower_own, upper)).astype(BF)
    twice = (once.astype(F32) - matmul(lower_second, upper_second)).astype(BF)
    return upper, following, jnp.where(me == 0, upper, jnp.where(me == 1, upper_second, twice))


def choose_kernel(reach, old, more, new, newer, *halves):
    my_col = lax.axis_index("col")
    fresh = jnp.logical_and(my_col >= reach, my_col < 2 * reach)
    for out, stale, arrived in zip(halves, (old, more), (new, newer)):
        out[...] = jnp.where(fresh, arrived[...], stale[...])


def first_kernel(block, *refs):
    mine, theirs = refs[:2], refs[2:4]
    low, high, work, result, panels = refs[4:]
    even = lax.rem(lax.axis_index("col"), 2) == 0
    lower_own, lower_next = [jnp.where(even, x[...], y[...]) for x, y in zip(mine, theirs)]
    second_own, head = [jnp.where(even, y[...], x[...]) for x, y in zip(mine, theirs)]
    me = lax.axis_index("row")
    top, own = work.at[: 2 * block], work.at[2 * block :]
    panel = (second_own.astype(F32) - matmul(lower_own, head)).astype(BF)
    lower_second = rounded(panel, high[1])
    panels[:block] = lower_own
    panels[block : 2 * block] = lower_next
    panels[2 * block :] = lower_second
    upper, following, final = finish(block, me, lower_own, lower_next, lower_second, low, top, own)
    result[...] = final

    @pl.when(lax.axis_index("col") == 0)
    def _():
        result[:, :block] = jnp.where(me == 0, top[:block, :block], lower_own)

    @pl.when(lax.axis_index("col") == 1)
    def _():
        rest = jnp.where(me == 1, following[:, :block], lower_second)
        result[:, :block] = jnp.where(me == 0, upper[:, :block], rest)


def columns(base, width, quarters):
    place = lax.rem(lax.axis_index("row"), 4)
    return [pl.multiple_of(base + lax.bitwise_xor(place, d) * width, LANES) for d in quarters]


def sends(result, out, starts, width, done, first):
    copies = []
    for i, start in enumerate(starts):
        piece = result.at[:, pl.ds(i * width, width)]
        copies.append(pltpu.make_async_copy(piece, out.at[:, pl.ds(start, width)], done.at[first + i]))
        copies[i].start()
    return copies


def later_kernel(block, last, chunk, quarters, earlier, foreign, kept, mine, put, raw, panels, low, ready, *refs):
    count = len(quarters)
    messages = refs[:count]
    out, *result, rows, slots, top, own, done = refs[count + (earlier is not None) :]
    result = result[0]
    base, width = chunk
    me = lax.axis_index("row")
    if earlier is None:
        copies = sends(ready, out, [0], ready.shape[1], done, 0)
    else:
        copies = sends(ready, out, columns(*earlier), earlier[1], done, 0)
    starts = columns(base, width, quarters)
    for i, start in enumerate(starts):
        rows[:, i * width : (i + 1) * width] = raw[:, pl.ds(start, width)]
        slots[:, i * width : (i + 1) * width] = messages[i][...]
    settle(block, me, foreign, kept, mine, put, rows[...], slots, top, own)
    _, _, final = finish(block, me, panels[:block], panels[block : 2 * block], panels[2 * block :], low, top, own)
    result[...] = final
    if last:
        copies += sends(result, out, starts, width, done, len(copies))
    for copy in copies:
        copy.wait()


def exchange(value, bit, axis="row"):
    return lax.ppermute(value, axis, [(i, i ^ bit) for i in range(lax.axis_size(axis))])


def body(matrix, pivots, lower_inverse, upper_inverse):
    rows, cols = matrix.shape
    block = lower_inverse.shape[1]
    grid_rows = lax.axis_size("row")
    grid_cols = lax.axis_size("col")
    my_row = lax.axis_index("row")
    my_col = lax.axis_index("col")
    units = cols // (4 * LANES)
    widths = [1, units - 1]
    chunks = []
    base = 0
    for count in widths:
        chunks.append((base, count * LANES))
        base += 4 * count * LANES
    groups = grid_rows // 4
    last_side = max(groups // 2, 1)
    shape = jax.ShapeDtypeStruct

    def spread(chunk, after=()):
        base, width = chunk
        span = 4 * width
        source, spec = matrix, WHOLE
        if base == 0:
            source = pltpu.with_memory_space_constraint(matrix, pltpu.HBM)
            spec = pl.BlockSpec((rows, span), lambda step: (0, 0))
        mine, near, far, across = call(
            functools.partial(pack_kernel, base, width),
            [shape((rows, width), BF)] * 4,
            [spec],
            [WHOLE] * 4,
            source,
            after=after,
        )
        return [mine, exchange(near, 1), exchange(far, 2), exchange(across, 3)]

    gathered = spread(chunks[0])

    src, foreign, kept, gather, displaced, mine, put = call(
        functools.partial(plan_kernel, block),
        [
            shape((2 * block, LANES), I32),
            shape((2 * block, LANES), BF),
            shape((block, LANES), BF),
            shape((2 * block, 4 * block), BF),
            shape((2 * block, 2 * block), BF),
            shape((2 * block, block), BF),
            shape((block, 2 * block), BF),
        ],
        [WHOLE],
        [WHOLE] * 7,
        pivots,
    )

    owner_group = src[:, :1] // block // 4
    my_group = my_row // 4

    def collect(part, width, pieces, after=()):
        count = len(pieces)
        slots = [shape((size, width), BF) for size in pieces]
        outs = call(
            functools.partial(select_kernel, block, pieces),
            slots * 2,
            [WHOLE] * (2 + len(part)),
            [WHOLE] * (2 * count),
            gather,
            displaced,
            *part,
            after=after,
            scratch=[pltpu.VMEM((4 * block, width), BF)],
        )
        return outs[:count], outs[count:]

    def deliver(held, gone, width, after=()):
        pieces = [piece.shape[0] for piece in held]
        side = 1
        while side < last_side:
            received = [exchange(piece, 4 * side) for piece in held]
            here = my_group // side
            owners = [owner_group[rows] // side for rows in spans(pieces)]
            keep = [jnp.logical_or(o == here, jnp.logical_and(here == 0, o != 1)) for o in owners]
            gone = [jnp.where(here == 1, new, old) for new, old in zip(received, gone)]
            held = [jnp.where(k, old, new) for k, old, new in zip(keep, held, received)]
            side *= 2
        received = [exchange(piece, 4 * side) for piece in held]
        messages = call(
            functools.partial(merge_kernel, block, last_side, pieces),
            [shape((2 * block, width), BF)] * 4,
            [WHOLE] * (1 + 3 * len(pieces)),
            [WHOLE] * 4,
            src,
            *held,
            *received,
            *gone,
            after=after,
        )
        return [messages[0]] + [exchange(messages[d], d) for d in (1, 2, 3)]

    width = chunks[0][1]
    held, gone = collect(gathered, width, [2 * block])
    collected = [collect(spread(chunk, after=[mine]), chunk[1], [2 * block - 160, 160]) for chunk in chunks[1:]]
    first = deliver(held, gone, width, after=[c[0][0] for c in collected])

    base, width = chunks[0]
    span = 4 * width
    work, *sent = call(
        functools.partial(panel_kernel, block, base, width),
        [shape((3 * block, span), BF)] + [shape((block, block), BF)] * 2,
        [WHOLE] * 11,
        [WHOLE] * 3,
        foreign,
        kept,
        mine,
        put,
        *first,
        matrix,
        lower_inverse,
        upper_inverse,
        scratch=[pltpu.VMEM((2 * block, span), BF)],
    )
    messages = [deliver(*c, width, after=sent[:1]) for c, (_, width) in zip(collected, chunks[1:])]
    reach = 2
    halved = sent
    halves = [shape((block, block), BF)] * 2
    while reach < grid_cols:
        arrived = [exchange(part, reach, "col") for part in sent]
        halved = call(functools.partial(choose_kernel, reach), halves, [WHOLE] * 4, [WHOLE] * 2, *sent, *arrived)
        reach *= 2
        if reach < grid_cols:
            sent = halved
    other = [exchange(part, 1, "col") for part in halved]

    ready, panels = call(
        functools.partial(first_kernel, block),
        [shape((block, span), BF), shape((3 * block, block), BF)],
        [WHOLE] * 7,
        [WHOLE, WHOLE],
        *halved,
        *other,
        lower_inverse,
        upper_inverse,
        work,
    )
    stages = [(k, quarters) for k in range(1, len(chunks)) for quarters in ((0, 1, 2), (3,))]
    earlier, out = None, []
    for index, (k, quarters) in enumerate(stages):
        last = index == len(stages) - 1
        count = len(quarters)
        base, width = chunks[k]
        span = count * width
        result = shape((block, span), BF)
        scratch = [
            pltpu.VMEM((block, span), BF),
            pltpu.VMEM((2 * block, span), BF),
            pltpu.VMEM((2 * block, span), BF),
            pltpu.VMEM((block, span), BF),
            pltpu.SemaphoreType.DMA((8,)),
        ]
        out, *results = call(
            functools.partial(later_kernel, block, last, chunks[k], quarters, earlier),
            [shape((rows, cols), BF)] + [result] * (not last),
            [WHOLE] * (8 + count) + [ANYWHERE] * len(out),
            [ANYWHERE] + [WHOLE] * (not last),
            foreign,
            kept,
            mine,
            put,
            matrix,
            panels,
            lower_inverse,
            ready,
            *[messages[k - 1][d] for d in quarters],
            *out,
            aliases={8 + count: 0} if out else {},
            scratch=[pltpu.VMEM((block, span), BF)] * last + scratch,
        )
        earlier = (base, width, quarters)
        ready, out = (results or [None])[0], [out]
    return out[0]


def solution(mesh):
    placed = (P("row", "col"), P(), P(), P())
    return jax.shard_map(
        body, mesh=mesh, in_specs=placed, out_specs=P("row", "col"), check_vma=False
    )
```

```python
import functools

import jax
import jax.numpy as jnp
from jax import lax
from jax.experimental import pallas as pl
from jax.experimental.pallas import tpu as pltpu
from jax.sharding import PartitionSpec as P

BF = jnp.bfloat16
F32 = jnp.float32
I32 = jnp.int32
VMEM_LIMIT = 12 * 1024 * 1024
LANES = 128
ANYWHERE = pl.BlockSpec(memory_space=pl.ANY)
WHOLE = pl.BlockSpec(memory_space=pltpu.VMEM)
PARAMS = pltpu.CompilerParams(vmem_limit_bytes=VMEM_LIMIT)


def matmul(a, b):
    return jnp.dot(a, b, preferred_element_type=F32)


def rounded(a, b):
    return matmul(a, b).astype(BF)


def call(kernel, out_shape, in_specs, out_specs, *args, after=(), aliases=None, scratch=(), flops=1 << 27):
    moved = sum(a.size * a.dtype.itemsize for a in args)
    used = len(args)

    def ordered(*refs):
        kernel(*refs[:used], *refs[used + len(after) :])

    in_specs = list(in_specs) + [ANYWHERE] * len(after)
    args = args + tuple(after)
    return pl.pallas_call(
        ordered,
        grid=(1,),
        out_shape=out_shape,
        in_specs=in_specs,
        out_specs=out_specs,
        scratch_shapes=list(scratch),
        input_output_aliases=aliases or {},
        compiler_params=PARAMS,
        cost_estimate=pl.CostEstimate(flops=flops, bytes_accessed=moved, transcendentals=0),
    )(*args)


def pack_kernel(base, width, source, *outs):
    place = lax.rem(lax.axis_index("row"), 4)
    for d in range(4):
        start = pl.multiple_of(base + lax.bitwise_xor(place, d) * width, LANES)
        outs[d][...] = source[:, pl.ds(start, width)]


def pick(flags, values, axis):
    return jnp.sum(jnp.where(flags, values, 0.0), axis=axis, keepdims=True)


def found(flags, axis):
    return jnp.max(jnp.where(flags, 1.0, 0.0), axis=axis, keepdims=True) > 0.0


def plan_kernel(block, flat, src_out, foreign_out, kept_out, gather_out, displaced_out, mine_out, put_out):
    me = lax.axis_index("row")
    first_row = flat[0:1, :].astype(F32)
    second_row = flat[1:2, :].astype(F32)
    shape = (block, block)
    down = lax.broadcasted_iota(I32, shape, 0).astype(F32)
    along = lax.broadcasted_iota(I32, shape, 1).astype(F32)
    first_col = pick(down == along, first_row, 1)
    second_col = pick(down == along, second_row, 1)
    size = float(block)
    both = first_col == second_row
    both_turned = second_col == first_row
    inside = first_col == along + size
    inside_turned = first_row == down + size
    moved_row = jnp.where(found(inside, 0), pick(inside, down, 0), along[0:1] + size)
    moved_col = jnp.where(found(inside_turned, 1), pick(inside_turned, along, 1), down[:, 0:1] + size)
    source_row = jnp.where(found(both, 0), pick(both, down, 0), second_row)
    source_col = jnp.where(found(both_turned, 1), pick(both_turned, along, 1), second_col)
    shifted_col = jnp.where(found(both, 1), pick(both, moved_row, 1), down[:, 0:1])
    sources = jnp.concatenate([first_col, source_col], axis=0).astype(I32)
    displaced = jnp.concatenate([shifted_col, moved_col], axis=0).astype(I32)
    source_flat = jnp.concatenate([first_row, source_row], axis=1).astype(I32)
    src_out[...] = jnp.broadcast_to(sources, src_out.shape)
    square = me - lax.rem(me, 4)
    here = jnp.logical_and(sources >= square * block, sources < (square + 4) * block)
    leaves = sources >= 2 * block
    at_home = square == 0
    taken = jnp.where(here, sources, jnp.where(at_home, displaced, -1))
    gone = jnp.where(jnp.logical_and(leaves, at_home), displaced, -1)
    lanes = lax.broadcasted_iota(I32, (2 * block, block), 1)
    for d in range(4):
        cols = slice(d * block, (d + 1) * block)
        gather_out[:, cols] = jnp.where(taken - lax.bitwise_xor(me, d) * block == lanes, 1.0, 0.0).astype(BF)
    near = jnp.where(lax.rem(me, 4) < 2, 0, 2)
    for d in range(2):
        cols = slice(d * block, (d + 1) * block)
        base = lax.bitwise_xor(me, near + d) * block
        displaced_out[:, cols] = jnp.where(gone - base == lanes, 1.0, 0.0).astype(BF)
    mine_out[...] = jnp.where(sources - me * block == lanes, 1.0, 0.0).astype(BF)
    rows = lax.broadcasted_iota(I32, (block, 2 * block), 0) + me * block
    put = source_flat == rows
    put_out[...] = jnp.where(put, 1.0, 0.0).astype(BF)
    kept_out[...] = jnp.broadcast_to(jnp.where(found(put, 1), 0.0, 1.0), kept_out.shape).astype(BF)
    owned = jnp.logical_and(sources >= me * block, sources < (me + 1) * block)
    foreign_out[...] = jnp.broadcast_to(jnp.where(owned, 0.0, 1.0), foreign_out.shape).astype(BF)


def spans(sizes):
    return [slice(sum(sizes[:i]), sum(sizes[: i + 1])) for i in range(len(sizes))]


def select_kernel(block, pieces, gather, displaced, *refs):
    count = len(pieces)
    parts, rows = refs[: -2 * count - 1], refs[-1]
    kept, gone = refs[-2 * count - 1 : -count - 1], refs[-count - 1 : -1]
    start = 0
    for part in parts:
        rows[start : start + part.shape[0]] = part[...]
        start += part.shape[0]
    start = pl.multiple_of(jnp.where(lax.rem(lax.axis_index("row"), 4) < 2, 0, 2 * block), 2 * block)
    for i, slots in enumerate(spans(pieces)):
        kept[i][...] = rounded(gather[slots], rows[...])
        gone[i][...] = rounded(displaced[slots], rows[pl.ds(start, 2 * block)])


def tiles(width):
    return [slice(i, i + LANES) for i in range(0, width, LANES)]


def merge_kernel(block, last_side, pieces, src, *refs):
    count = len(pieces)
    kept, received, gone = refs[:count], refs[count : 2 * count], refs[2 * count : 3 * count]
    outs = refs[3 * count :]
    me = lax.axis_index("row")
    side = 4 * last_side
    mine = lax.div(me, side) * side * block
    low_side = me < side
    for i, rows in enumerate(spans(pieces)):
        sources = src[rows]
        from_here = jnp.logical_and(sources >= mine, sources < mine + side * block)
        leaves = sources >= 2 * block
        theirs = []
        for d in range(4):
            base = lax.bitwise_xor(me, d) * block
            theirs.append(jnp.logical_and(jnp.logical_and(sources >= base, sources < base + block), leaves))
        for cols in tiles(kept[i].shape[1]):
            arrived = received[i][:, cols].astype(F32)
            top = jnp.where(from_here, kept[i][:, cols].astype(F32), arrived)
            moved = jnp.where(low_side, gone[i][:, cols].astype(F32), arrived)
            for d in range(4):
                outs[d][rows, cols] = jnp.where(theirs[d], moved, top).astype(BF)


def settle(block, me, foreign, kept, candidates, put, here, slots, top, own):
    placed = rounded(put[...], slots[...])
    outside = foreign[...] > 0
    unmoved = kept[...] > 0
    for cols in tiles(here.shape[1]):
        top[:, cols] = jnp.where(outside, slots[:, cols], candidates[:, cols])
        own[:, cols] = jnp.where(unmoved, here[:, cols], placed[:, cols])

    @pl.when(me < 2)
    def _():
        own[...] = top[pl.ds(pl.multiple_of(jnp.minimum(me, 1) * block, block), block)]


def assemble(block, base, width, me, foreign, kept, mine, put, messages, raw, slots, top, own):
    place = lax.rem(me, 4)
    for d in range(4):
        start = pl.multiple_of(lax.bitwise_xor(place, d) * width, LANES)
        slots[:, pl.ds(start, width)] = messages[d][...]
    here = raw[:, base : base + 4 * width]
    settle(block, me, foreign, kept, rounded(mine[...], here), put, here, slots, top, own)


def panel_kernel(block, base, width, foreign, kept, mine, put, m0, m1, m2, m3, raw, low, high, work, sent, more, slots):
    top, own = work.at[: 2 * block], work.at[2 * block :]
    assemble(block, base, width, lax.axis_index("row"), foreign, kept, mine, put, (m0, m1, m2, m3), raw, slots, top, own)

    @pl.when(lax.axis_index("col") == 0)
    def _():
        sent[...] = rounded(own[:, :block], high[0])
        more[...] = rounded(top[block:, :block], high[0])

    @pl.when(lax.axis_index("col") != 0)
    def _():
        sent[...] = own[:, :block]
        more[...] = rounded(low[0], top[:block, :block])


def finish(block, me, lower_own, lower_next, lower_second, low, top, own):
    upper = rounded(low[0], top[:block])
    following = (top[block:].astype(F32) - matmul(lower_next, upper)).astype(BF)
    upper_second = rounded(low[1], following)
    once = (own[...].astype(F32) - matmul(lower_own, upper)).astype(BF)
    twice = (once.astype(F32) - matmul(lower_second, upper_second)).astype(BF)
    return upper, following, jnp.where(me == 0, upper, jnp.where(me == 1, upper_second, twice))


def choose_kernel(reach, old, more, new, newer, *halves):
    my_col = lax.axis_index("col")
    fresh = jnp.logical_and(my_col >= reach, my_col < 2 * reach)
    for out, stale, arrived in zip(halves, (old, more), (new, newer)):
        out[...] = jnp.where(fresh, arrived[...], stale[...])


def first_kernel(block, chunk, quarters, *refs):
    mine, theirs = refs[:2], refs[2:4]
    low, high, work, mine_rows, raw, result, panels, candidates = refs[4:]
    width = chunk[1]
    for i, start in enumerate(columns(*chunk, quarters)):
        candidates[:, i * width : (i + 1) * width] = rounded(mine_rows[...], raw[:, pl.ds(start, width)])
    even = lax.rem(lax.axis_index("col"), 2) == 0
    lower_own, lower_next = [jnp.where(even, x[...], y[...]) for x, y in zip(mine, theirs)]
    second_own, head = [jnp.where(even, y[...], x[...]) for x, y in zip(mine, theirs)]
    me = lax.axis_index("row")
    top, own = work.at[: 2 * block], work.at[2 * block :]
    panel = (second_own.astype(F32) - matmul(lower_own, head)).astype(BF)
    lower_second = rounded(panel, high[1])
    panels[:block] = lower_own
    panels[block : 2 * block] = lower_next
    panels[2 * block :] = lower_second
    upper, following, final = finish(block, me, lower_own, lower_next, lower_second, low, top, own)
    result[...] = final

    @pl.when(lax.axis_index("col") == 0)
    def _():
        result[:, :block] = jnp.where(me == 0, top[:block, :block], lower_own)

    @pl.when(lax.axis_index("col") == 1)
    def _():
        rest = jnp.where(me == 1, following[:, :block], lower_second)
        result[:, :block] = jnp.where(me == 0, upper[:, :block], rest)


def columns(base, width, quarters):
    place = lax.rem(lax.axis_index("row"), 4)
    return [pl.multiple_of(base + lax.bitwise_xor(place, d) * width, LANES) for d in quarters]


def sends(result, out, starts, width, done, first):
    copies = []
    for i, start in enumerate(starts):
        piece = result.at[:, pl.ds(i * width, width)]
        copies.append(pltpu.make_async_copy(piece, out.at[:, pl.ds(start, width)], done.at[first + i]))
        copies[i].start()
    return copies


def later_kernel(block, last, chunk, quarters, earlier, foreign, kept, mine, put, raw, panels, low, ready, *refs):
    count = len(quarters)
    messages = refs[:count]
    out, *result, rows, slots, top, own, done = refs[count + (earlier is not None) :]
    result = result[0]
    base, width = chunk
    me = lax.axis_index("row")
    if earlier is None:
        copies = sends(ready, out, [0], ready.shape[1], done, 0)
    else:
        copies = sends(ready, out, columns(*earlier), earlier[1], done, 0)
    starts = columns(base, width, quarters)
    for i, start in enumerate(starts):
        rows[:, i * width : (i + 1) * width] = raw[:, pl.ds(start, width)]
        slots[:, i * width : (i + 1) * width] = messages[i][...]
    candidates = mine[...] if last else rounded(mine[...], rows[...])
    settle(block, me, foreign, kept, candidates, put, rows[...], slots, top, own)
    _, _, final = finish(block, me, panels[:block], panels[block : 2 * block], panels[2 * block :], low, top, own)
    result[...] = final
    if last:
        copies += sends(result, out, starts, width, done, len(copies))
    for copy in copies:
        copy.wait()


def exchange(value, bit, axis="row"):
    return lax.ppermute(value, axis, [(i, i ^ bit) for i in range(lax.axis_size(axis))])


def body(matrix, pivots, lower_inverse, upper_inverse):
    rows, cols = matrix.shape
    block = lower_inverse.shape[1]
    grid_rows = lax.axis_size("row")
    grid_cols = lax.axis_size("col")
    my_row = lax.axis_index("row")
    my_col = lax.axis_index("col")
    units = cols // (4 * LANES)
    widths = [1, units - 1]
    chunks = []
    base = 0
    for count in widths:
        chunks.append((base, count * LANES))
        base += 4 * count * LANES
    groups = grid_rows // 4
    last_side = max(groups // 2, 1)
    shape = jax.ShapeDtypeStruct

    def spread(chunk, after=()):
        mine, near, far, across = call(
            functools.partial(pack_kernel, *chunk),
            [shape((rows, chunk[1]), BF)] * 4,
            [WHOLE],
            [WHOLE] * 4,
            matrix,
            after=after,
        )
        return [mine, exchange(near, 1), exchange(far, 2), exchange(across, 3)]

    gathered = spread(chunks[0])

    src, foreign, kept, gather, displaced, mine, put = call(
        functools.partial(plan_kernel, block),
        [
            shape((2 * block, LANES), I32),
            shape((2 * block, LANES), BF),
            shape((block, LANES), BF),
            shape((2 * block, 4 * block), BF),
            shape((2 * block, 2 * block), BF),
            shape((2 * block, block), BF),
            shape((block, 2 * block), BF),
        ],
        [WHOLE],
        [WHOLE] * 7,
        pivots,
    )

    owner_group = src[:, :1] // block // 4
    my_group = my_row // 4

    def collect(part, width, pieces, after=()):
        count = len(pieces)
        slots = [shape((size, width), BF) for size in pieces]
        outs = call(
            functools.partial(select_kernel, block, pieces),
            slots * 2,
            [WHOLE] * (2 + len(part)),
            [WHOLE] * (2 * count),
            gather,
            displaced,
            *part,
            after=after,
            scratch=[pltpu.VMEM((4 * block, width), BF)],
        )
        return outs[:count], outs[count:]

    def deliver(held, gone, width, after=()):
        pieces = [piece.shape[0] for piece in held]
        side = 1
        while side < last_side:
            received = [exchange(piece, 4 * side) for piece in held]
            here = my_group // side
            owners = [owner_group[rows] // side for rows in spans(pieces)]
            keep = [jnp.logical_or(o == here, jnp.logical_and(here == 0, o != 1)) for o in owners]
            gone = [jnp.where(here == 1, new, old) for new, old in zip(received, gone)]
            held = [jnp.where(k, old, new) for k, old, new in zip(keep, held, received)]
            side *= 2
        received = [exchange(piece, 4 * side) for piece in held]
        messages = call(
            functools.partial(merge_kernel, block, last_side, pieces),
            [shape((2 * block, width), BF)] * 4,
            [WHOLE] * (1 + 3 * len(pieces)),
            [WHOLE] * 4,
            src,
            *held,
            *received,
            *gone,
            after=after,
        )
        return [messages[0]] + [exchange(messages[d], d) for d in (1, 2, 3)]

    width = chunks[0][1]
    held, gone = collect(gathered, width, [2 * block])
    collected = [collect(spread(chunk, after=[mine]), chunk[1], [2 * block - 160, 160]) for chunk in chunks[1:]]
    first = deliver(held, gone, width, after=[c[0][0] for c in collected])

    base, width = chunks[0]
    span = 4 * width
    work, *sent = call(
        functools.partial(panel_kernel, block, base, width),
        [shape((3 * block, span), BF)] + [shape((block, block), BF)] * 2,
        [WHOLE] * 11,
        [WHOLE] * 3,
        foreign,
        kept,
        mine,
        put,
        *first,
        matrix,
        lower_inverse,
        upper_inverse,
        scratch=[pltpu.VMEM((2 * block, span), BF)],
    )
    messages = [deliver(*c, width, after=sent[:1]) for c, (_, width) in zip(collected, chunks[1:])]
    reach = 2
    halved = sent
    halves = [shape((block, block), BF)] * 2
    while reach < grid_cols:
        arrived = [exchange(part, reach, "col") for part in sent]
        halved = call(functools.partial(choose_kernel, reach), halves, [WHOLE] * 4, [WHOLE] * 2, *sent, *arrived)
        reach *= 2
        if reach < grid_cols:
            sent = halved
    other = [exchange(part, 1, "col") for part in halved]

    stages = [(k, quarters) for k in range(1, len(chunks)) for quarters in ((0, 1, 2), (3,))]
    final = stages[-1]
    last_width = chunks[final[0]][1] * len(final[1])
    ready, panels, candidates = call(
        functools.partial(first_kernel, block, chunks[final[0]], final[1]),
        [shape((block, span), BF), shape((3 * block, block), BF), shape((2 * block, last_width), BF)],
        [WHOLE] * 9,
        [WHOLE] * 3,
        *halved,
        *other,
        lower_inverse,
        upper_inverse,
        work,
        mine,
        matrix,
    )
    earlier, out = None, []
    for index, (k, quarters) in enumerate(stages):
        last = index == len(stages) - 1
        count = len(quarters)
        base, width = chunks[k]
        span = count * width
        result = shape((block, span), BF)
        scratch = [
            pltpu.VMEM((block, span), BF),
            pltpu.VMEM((2 * block, span), BF),
            pltpu.VMEM((2 * block, span), BF),
            pltpu.VMEM((block, span), BF),
            pltpu.SemaphoreType.DMA((8,)),
        ]
        out, *results = call(
            functools.partial(later_kernel, block, last, chunks[k], quarters, earlier),
            [shape((rows, cols), BF)] + [result] * (not last),
            [WHOLE] * (8 + count) + [ANYWHERE] * len(out),
            [ANYWHERE] + [WHOLE] * (not last),
            foreign,
            kept,
            candidates if last else mine,
            put,
            matrix,
            panels,
            lower_inverse,
            ready,
            *[messages[k - 1][d] for d in quarters],
            *out,
            aliases={8 + count: 0} if out else {},
            scratch=[pltpu.VMEM((block, span), BF)] * last + scratch,
        )
        earlier = (base, width, quarters)
        ready, out = (results or [None])[0], [out]
    return out[0]


def solution(mesh):
    placed = (P("row", "col"), P(), P(), P())
    return jax.shard_map(
        body, mesh=mesh, in_specs=placed, out_specs=P("row", "col"), check_vma=False
    )
```

```python
import functools

import jax
import jax.numpy as jnp
from jax import lax
from jax.experimental import pallas as pl
from jax.experimental.pallas import tpu as pltpu
from jax.sharding import PartitionSpec as P

BF = jnp.bfloat16
F32 = jnp.float32
I32 = jnp.int32
VMEM_LIMIT = 12 * 1024 * 1024
LANES = 128
ANYWHERE = pl.BlockSpec(memory_space=pl.ANY)
WHOLE = pl.BlockSpec(memory_space=pltpu.VMEM)
PARAMS = pltpu.CompilerParams(vmem_limit_bytes=VMEM_LIMIT)


def matmul(a, b):
    return jnp.dot(a, b, preferred_element_type=F32)


def rounded(a, b):
    return matmul(a, b).astype(BF)


def call(kernel, out_shape, in_specs, out_specs, *args, after=(), aliases=None, scratch=(), flops=1 << 27):
    moved = sum(a.size * a.dtype.itemsize for a in args)
    used = len(args)

    def ordered(*refs):
        kernel(*refs[:used], *refs[used + len(after) :])

    in_specs = list(in_specs) + [ANYWHERE] * len(after)
    args = args + tuple(after)
    return pl.pallas_call(
        ordered,
        grid=(1,),
        out_shape=out_shape,
        in_specs=in_specs,
        out_specs=out_specs,
        scratch_shapes=list(scratch),
        input_output_aliases=aliases or {},
        compiler_params=PARAMS,
        cost_estimate=pl.CostEstimate(flops=flops, bytes_accessed=moved, transcendentals=0),
    )(*args)


def pack_kernel(base, width, source, *outs):
    place = lax.rem(lax.axis_index("row"), 4)
    for d in range(4):
        start = pl.multiple_of(base + lax.bitwise_xor(place, d) * width, LANES)
        outs[d][...] = source[:, pl.ds(start, width)]


def pick(flags, values, axis):
    return jnp.sum(jnp.where(flags, values, 0.0), axis=axis, keepdims=True)


def found(flags, axis):
    return jnp.max(jnp.where(flags, 1.0, 0.0), axis=axis, keepdims=True) > 0.0


def plan_kernel(block, flat, src_out, foreign_out, kept_out, gather_out, displaced_out, mine_out, put_out):
    me = lax.axis_index("row")
    first_row = flat[0:1, :].astype(F32)
    second_row = flat[1:2, :].astype(F32)
    shape = (block, block)
    down = lax.broadcasted_iota(I32, shape, 0).astype(F32)
    along = lax.broadcasted_iota(I32, shape, 1).astype(F32)
    first_col = pick(down == along, first_row, 1)
    second_col = pick(down == along, second_row, 1)
    size = float(block)
    both = first_col == second_row
    both_turned = second_col == first_row
    inside = first_col == along + size
    inside_turned = first_row == down + size
    moved_row = jnp.where(found(inside, 0), pick(inside, down, 0), along[0:1] + size)
    moved_col = jnp.where(found(inside_turned, 1), pick(inside_turned, along, 1), down[:, 0:1] + size)
    source_row = jnp.where(found(both, 0), pick(both, down, 0), second_row)
    source_col = jnp.where(found(both_turned, 1), pick(both_turned, along, 1), second_col)
    shifted_col = jnp.where(found(both, 1), pick(both, moved_row, 1), down[:, 0:1])
    sources = jnp.concatenate([first_col, source_col], axis=0).astype(I32)
    displaced = jnp.concatenate([shifted_col, moved_col], axis=0).astype(I32)
    source_flat = jnp.concatenate([first_row, source_row], axis=1).astype(I32)
    src_out[...] = jnp.broadcast_to(sources, src_out.shape)
    square = me - lax.rem(me, 4)
    here = jnp.logical_and(sources >= square * block, sources < (square + 4) * block)
    leaves = sources >= 2 * block
    at_home = square == 0
    taken = jnp.where(here, sources, jnp.where(at_home, displaced, -1))
    gone = jnp.where(jnp.logical_and(leaves, at_home), displaced, -1)
    lanes = lax.broadcasted_iota(I32, (2 * block, block), 1)
    for d in range(4):
        cols = slice(d * block, (d + 1) * block)
        gather_out[:, cols] = jnp.where(taken - lax.bitwise_xor(me, d) * block == lanes, 1.0, 0.0).astype(BF)
    near = jnp.where(lax.rem(me, 4) < 2, 0, 2)
    for d in range(2):
        cols = slice(d * block, (d + 1) * block)
        base = lax.bitwise_xor(me, near + d) * block
        displaced_out[:, cols] = jnp.where(gone - base == lanes, 1.0, 0.0).astype(BF)
    mine_out[...] = jnp.where(sources - me * block == lanes, 1.0, 0.0).astype(BF)
    rows = lax.broadcasted_iota(I32, (block, 2 * block), 0) + me * block
    put = source_flat == rows
    put_out[...] = jnp.where(put, 1.0, 0.0).astype(BF)
    kept_out[...] = jnp.broadcast_to(jnp.where(found(put, 1), 0.0, 1.0), kept_out.shape).astype(BF)
    owned = jnp.logical_and(sources >= me * block, sources < (me + 1) * block)
    foreign_out[...] = jnp.broadcast_to(jnp.where(owned, 0.0, 1.0), foreign_out.shape).astype(BF)


def spans(sizes):
    return [slice(sum(sizes[:i]), sum(sizes[: i + 1])) for i in range(len(sizes))]


def select_kernel(block, pieces, gather, displaced, *refs):
    count = len(pieces)
    parts, rows = refs[: -2 * count - 1], refs[-1]
    kept, gone = refs[-2 * count - 1 : -count - 1], refs[-count - 1 : -1]
    start = 0
    for part in parts:
        rows[start : start + part.shape[0]] = part[...]
        start += part.shape[0]
    start = pl.multiple_of(jnp.where(lax.rem(lax.axis_index("row"), 4) < 2, 0, 2 * block), 2 * block)
    for i, slots in enumerate(spans(pieces)):
        kept[i][...] = rounded(gather[slots], rows[...])
        gone[i][...] = rounded(displaced[slots], rows[pl.ds(start, 2 * block)])


def tiles(width):
    return [slice(i, i + LANES) for i in range(0, width, LANES)]


def merge_kernel(block, last_side, pieces, src, *refs):
    count = len(pieces)
    kept, received, gone = refs[:count], refs[count : 2 * count], refs[2 * count : 3 * count]
    outs = refs[3 * count :]
    me = lax.axis_index("row")
    side = 4 * last_side
    mine = lax.div(me, side) * side * block
    low_side = me < side
    for i, rows in enumerate(spans(pieces)):
        sources = src[rows]
        from_here = jnp.logical_and(sources >= mine, sources < mine + side * block)
        leaves = sources >= 2 * block
        theirs = []
        for d in range(4):
            base = lax.bitwise_xor(me, d) * block
            theirs.append(jnp.logical_and(jnp.logical_and(sources >= base, sources < base + block), leaves))
        for cols in tiles(kept[i].shape[1]):
            arrived = received[i][:, cols].astype(F32)
            top = jnp.where(from_here, kept[i][:, cols].astype(F32), arrived)
            moved = jnp.where(low_side, gone[i][:, cols].astype(F32), arrived)
            for d in range(4):
                outs[d][rows, cols] = jnp.where(theirs[d], moved, top).astype(BF)


def settle(block, me, foreign, kept, candidates, put, here, slots, top, own):
    placed = rounded(put[...], slots[...])
    outside = foreign[...] > 0
    unmoved = kept[...] > 0
    for cols in tiles(here.shape[1]):
        top[:, cols] = jnp.where(outside, slots[:, cols], candidates[:, cols])
        own[:, cols] = jnp.where(unmoved, here[:, cols], placed[:, cols])

    @pl.when(me < 2)
    def _():
        own[...] = top[pl.ds(pl.multiple_of(jnp.minimum(me, 1) * block, block), block)]


def assemble(block, base, width, me, foreign, kept, mine, put, messages, raw, slots, top, own):
    place = lax.rem(me, 4)
    for d in range(4):
        start = pl.multiple_of(lax.bitwise_xor(place, d) * width, LANES)
        slots[:, pl.ds(start, width)] = messages[d][...]
    here = raw[:, base : base + 4 * width]
    settle(block, me, foreign, kept, rounded(mine[...], here), put, here, slots, top, own)


def panel_kernel(block, base, width, foreign, kept, mine, put, m0, m1, m2, m3, raw, low, high, work, sent, more, slots):
    top, own = work.at[: 2 * block], work.at[2 * block :]
    assemble(block, base, width, lax.axis_index("row"), foreign, kept, mine, put, (m0, m1, m2, m3), raw, slots, top, own)

    @pl.when(lax.axis_index("col") == 0)
    def _():
        sent[...] = rounded(own[:, :block], high[0])
        more[...] = rounded(top[block:, :block], high[0])

    @pl.when(lax.axis_index("col") != 0)
    def _():
        sent[...] = own[:, :block]
        more[...] = rounded(low[0], top[:block, :block])


def finish(block, me, lower_own, lower_next, lower_second, low, top, own):
    upper = rounded(low[0], top[:block])
    following = (top[block:].astype(F32) - matmul(lower_next, upper)).astype(BF)
    upper_second = rounded(low[1], following)
    once = (own[...].astype(F32) - matmul(lower_own, upper)).astype(BF)
    twice = (once.astype(F32) - matmul(lower_second, upper_second)).astype(BF)
    return upper, following, jnp.where(me == 0, upper, jnp.where(me == 1, upper_second, twice))


def choose_kernel(reach, old, more, new, newer, *halves):
    my_col = lax.axis_index("col")
    fresh = jnp.logical_and(my_col >= reach, my_col < 2 * reach)
    for out, stale, arrived in zip(halves, (old, more), (new, newer)):
        out[...] = jnp.where(fresh, arrived[...], stale[...])


def first_kernel(block, chunk, quarters, *refs):
    mine, theirs = refs[:2], refs[2:4]
    low, high, work, mine_rows, raw, result, panels, candidates = refs[4:]
    width = chunk[1]
    for i, start in enumerate(columns(*chunk, quarters)):
        candidates[:, i * width : (i + 1) * width] = rounded(mine_rows[...], raw[:, pl.ds(start, width)])
    even = lax.rem(lax.axis_index("col"), 2) == 0
    lower_own, lower_next = [jnp.where(even, x[...], y[...]) for x, y in zip(mine, theirs)]
    second_own, head = [jnp.where(even, y[...], x[...]) for x, y in zip(mine, theirs)]
    me = lax.axis_index("row")
    top, own = work.at[: 2 * block], work.at[2 * block :]
    panel = (second_own.astype(F32) - matmul(lower_own, head)).astype(BF)
    lower_second = rounded(panel, high[1])
    panels[:block] = lower_own
    panels[block : 2 * block] = lower_next
    panels[2 * block :] = lower_second
    upper, following, final = finish(block, me, lower_own, lower_next, lower_second, low, top, own)
    result[...] = final

    @pl.when(lax.axis_index("col") == 0)
    def _():
        result[:, :block] = jnp.where(me == 0, top[:block, :block], lower_own)

    @pl.when(lax.axis_index("col") == 1)
    def _():
        rest = jnp.where(me == 1, following[:, :block], lower_second)
        result[:, :block] = jnp.where(me == 0, upper[:, :block], rest)


def columns(base, width, quarters):
    place = lax.rem(lax.axis_index("row"), 4)
    return [pl.multiple_of(base + lax.bitwise_xor(place, d) * width, LANES) for d in quarters]


def sends(result, out, starts, width, done, first):
    copies = []
    for i, start in enumerate(starts):
        piece = result.at[:, pl.ds(i * width, width)]
        copies.append(pltpu.make_async_copy(piece, out.at[:, pl.ds(start, width)], done.at[first + i]))
        copies[i].start()
    return copies


def later_kernel(block, last, chunk, quarters, earlier, foreign, kept, mine, put, raw, panels, low, ready, *refs):
    count = len(quarters)
    messages = refs[:count]
    out, *result, rows, slots, top, own, done = refs[count + (earlier is not None) :]
    result = result[0]
    base, width = chunk
    me = lax.axis_index("row")
    if earlier is None:
        copies = sends(ready, out, [0], ready.shape[1], done, 0)
    else:
        copies = sends(ready, out, columns(*earlier), earlier[1], done, 0)
    starts = columns(base, width, quarters)
    for i, start in enumerate(starts):
        rows[:, i * width : (i + 1) * width] = raw[:, pl.ds(start, width)]
        slots[:, i * width : (i + 1) * width] = messages[i][...]
    candidates = mine[...] if last else rounded(mine[...], rows[...])
    settle(block, me, foreign, kept, candidates, put, rows[...], slots, top, own)
    _, _, final = finish(block, me, panels[:block], panels[block : 2 * block], panels[2 * block :], low, top, own)
    result[...] = final
    if last:
        copies += sends(result, out, starts, width, done, len(copies))
    for copy in copies:
        copy.wait()


def exchange(value, bit, axis="row"):
    return lax.ppermute(value, axis, [(i, i ^ bit) for i in range(lax.axis_size(axis))])


def body(matrix, pivots, lower_inverse, upper_inverse):
    rows, cols = matrix.shape
    block = lower_inverse.shape[1]
    grid_rows = lax.axis_size("row")
    grid_cols = lax.axis_size("col")
    my_row = lax.axis_index("row")
    my_col = lax.axis_index("col")
    units = cols // (4 * LANES)
    widths = [1, units - 1]
    chunks = []
    base = 0
    for count in widths:
        chunks.append((base, count * LANES))
        base += 4 * count * LANES
    groups = grid_rows // 4
    last_side = max(groups // 2, 1)
    shape = jax.ShapeDtypeStruct

    def spread(chunk, after=()):
        base, width = chunk
        span = 4 * width
        source, spec = matrix, WHOLE
        if base == 0:
            source = pltpu.with_memory_space_constraint(matrix, pltpu.HBM)
            spec = pl.BlockSpec((rows, span), lambda step: (0, 0))
        mine, near, far, across = call(
            functools.partial(pack_kernel, base, width),
            [shape((rows, width), BF)] * 4,
            [spec],
            [WHOLE] * 4,
            source,
            after=after,
        )
        return [mine, exchange(near, 1), exchange(far, 2), exchange(across, 3)]

    gathered = spread(chunks[0])

    src, foreign, kept, gather, displaced, mine, put = call(
        functools.partial(plan_kernel, block),
        [
            shape((2 * block, LANES), I32),
            shape((2 * block, LANES), BF),
            shape((block, LANES), BF),
            shape((2 * block, 4 * block), BF),
            shape((2 * block, 2 * block), BF),
            shape((2 * block, block), BF),
            shape((block, 2 * block), BF),
        ],
        [WHOLE],
        [WHOLE] * 7,
        pivots,
    )

    owner_group = src[:, :1] // block // 4
    my_group = my_row // 4

    def collect(part, width, pieces, after=()):
        count = len(pieces)
        slots = [shape((size, width), BF) for size in pieces]
        outs = call(
            functools.partial(select_kernel, block, pieces),
            slots * 2,
            [WHOLE] * (2 + len(part)),
            [WHOLE] * (2 * count),
            gather,
            displaced,
            *part,
            after=after,
            scratch=[pltpu.VMEM((4 * block, width), BF)],
        )
        return outs[:count], outs[count:]

    def deliver(held, gone, width, after=()):
        pieces = [piece.shape[0] for piece in held]
        side = 1
        while side < last_side:
            received = [exchange(piece, 4 * side) for piece in held]
            here = my_group // side
            owners = [owner_group[rows] // side for rows in spans(pieces)]
            keep = [jnp.logical_or(o == here, jnp.logical_and(here == 0, o != 1)) for o in owners]
            gone = [jnp.where(here == 1, new, old) for new, old in zip(received, gone)]
            held = [jnp.where(k, old, new) for k, old, new in zip(keep, held, received)]
            side *= 2
        received = [exchange(piece, 4 * side) for piece in held]
        messages = call(
            functools.partial(merge_kernel, block, last_side, pieces),
            [shape((2 * block, width), BF)] * 4,
            [WHOLE] * (1 + 3 * len(pieces)),
            [WHOLE] * 4,
            src,
            *held,
            *received,
            *gone,
            after=after,
        )
        return [messages[0]] + [exchange(messages[d], d) for d in (1, 2, 3)]

    width = chunks[0][1]
    held, gone = collect(gathered, width, [2 * block])
    collected = [collect(spread(chunk, after=[mine]), chunk[1], [2 * block - 160, 160]) for chunk in chunks[1:]]
    first = deliver(held, gone, width, after=[c[0][0] for c in collected])

    base, width = chunks[0]
    span = 4 * width
    work, *sent = call(
        functools.partial(panel_kernel, block, base, width),
        [shape((3 * block, span), BF)] + [shape((block, block), BF)] * 2,
        [WHOLE] * 11,
        [WHOLE] * 3,
        foreign,
        kept,
        mine,
        put,
        *first,
        matrix,
        lower_inverse,
        upper_inverse,
        scratch=[pltpu.VMEM((2 * block, span), BF)],
    )
    messages = [deliver(*c, width, after=sent[:1]) for c, (_, width) in zip(collected, chunks[1:])]
    reach = 2
    halved = sent
    halves = [shape((block, block), BF)] * 2
    while reach < grid_cols:
        arrived = [exchange(part, reach, "col") for part in sent]
        halved = call(functools.partial(choose_kernel, reach), halves, [WHOLE] * 4, [WHOLE] * 2, *sent, *arrived)
        reach *= 2
        if reach < grid_cols:
            sent = halved
    other = [exchange(part, 1, "col") for part in halved]

    stages = [(k, quarters) for k in range(1, len(chunks)) for quarters in ((0, 1, 2), (3,))]
    final = stages[-1]
    last_width = chunks[final[0]][1] * len(final[1])
    ready, panels, candidates = call(
        functools.partial(first_kernel, block, chunks[final[0]], final[1]),
        [shape((block, span), BF), shape((3 * block, block), BF), shape((2 * block, last_width), BF)],
        [WHOLE] * 9,
        [WHOLE] * 3,
        *halved,
        *other,
        lower_inverse,
        upper_inverse,
        work,
        mine,
        matrix,
    )
    earlier, out = None, []
    for index, (k, quarters) in enumerate(stages):
        last = index == len(stages) - 1
        count = len(quarters)
        base, width = chunks[k]
        span = count * width
        result = shape((block, span), BF)
        scratch = [
            pltpu.VMEM((block, span), BF),
            pltpu.VMEM((2 * block, span), BF),
            pltpu.VMEM((2 * block, span), BF),
            pltpu.VMEM((block, span), BF),
            pltpu.SemaphoreType.DMA((8,)),
        ]
        out, *results = call(
            functools.partial(later_kernel, block, last, chunks[k], quarters, earlier),
            [shape((rows, cols), BF)] + [result] * (not last),
            [WHOLE] * (8 + count) + [ANYWHERE] * len(out),
            [ANYWHERE] + [WHOLE] * (not last),
            foreign,
            kept,
            candidates if last else mine,
            put,
            matrix,
            panels,
            lower_inverse,
            ready,
            *[messages[k - 1][d] for d in quarters],
            *out,
            aliases={8 + count: 0} if out else {},
            scratch=[pltpu.VMEM((block, span), BF)] * last + scratch,
        )
        earlier = (base, width, quarters)
        ready, out = (results or [None])[0], [out]
    return out[0]


def solution(mesh):
    placed = (P("row", "col"), P(), P(), P())
    return jax.shard_map(
        body, mesh=mesh, in_specs=placed, out_specs=P("row", "col"), check_vma=False
    )
```
